32 devices in a mesh: exa: 4 (over z), exb: 8 (over y, x, core).
Axes of the slice: x: 2, y: 2, z: 4, core: 2. Of those that a mesh axis runs over, the one named last changes fastest.
Arguments:
- features: float32 [262144, 128], P(('exa', 'exb')), may hold values from -6 to 6
- sign_bits: int32 [262144], P(('exa', 'exb')), may hold values from 0 to 1
- sample_device: int32 [16384, 1], replicated, may hold values from 0 to 31; in each aligned block of 512 rows (0 to 511, 512 to 1023, ...) at most 32 rows name the same one
- sample_offset: int32 [16384], replicated, may hold values from 0 to 8191, as said below
Outputs:
- q_rows: float32 [16384, 128], P(('exa', 'exb'))
- upper_factor: float32 [128, 128], replicated
The draws below stay inside these ranges and needn't reach their ends.
Inputs may be any that keep to these rules, and one draw needn't show every extreme that they name: `sample_device`: within each aligned block of 512 rows no value appears more than 32 times. `sample_offset`: within each aligned block of 512 rows, at most 32 values fall into any one range of 256 consecutive offsets that starts at a multiple of 256, and in every block some range holds exactly 32.
All inputs are finite; a program needn't handle non-finite values.
Results may differ from the reference program's by a relative error of at most 0.000071.
Values sent between devices are 32-bit elements; how exact they have to be, the bound alone decides.
No kernel may reach another device: no remote copies, remote signals or barrier semaphores. Data moves between devices by JAX's collectives and lax.ppermute only.
A program may use at most 64 MiB of HBM per device.

```python
import math
import jax
import jax.numpy as jnp
import numpy as np
from jax import lax

F = 128
L_DEV = 8192
K_DEV = 512
EXAMPLES = 262144
SAMPLES = 16384
MOST = 32
N_EXA = 4
N_EXB = 8
DEVICES = 32


def draw_sample_offset(key, part):
    group_rows = L_DEV // DEVICES
    capacity = max(4, 2 * K_DEV // DEVICES)

    def one_block(block_key):
        first_key, second_key, third_key, fourth_key = jax.random.split(block_key, 4)
        heavy = jax.random.randint(first_key, (), 0, DEVICES).astype(jnp.int32)
        others = jnp.arange((DEVICES - 1) * capacity, dtype=jnp.int32) // capacity
        others = (heavy + 1 + others) % DEVICES
        others = jax.random.permutation(second_key, others)[:K_DEV - capacity]
        groups = jnp.concatenate([jnp.full((capacity,), heavy, jnp.int32), others.astype(jnp.int32)])
        groups = jax.random.permutation(third_key, groups)
        within = jax.random.randint(fourth_key, (K_DEV,), 0, group_rows).astype(jnp.int32)
        return groups * group_rows + within
    block_keys = jax.random.split(jax.random.fold_in(key, 7), DEVICES)
    return jax.vmap(one_block)(block_keys).reshape(-1).astype(jnp.int32)


def with_ends(array, own_key, low, largest):
    longest = array.shape.index(max(array.shape))
    spots = []
    for shift in (0, 1):
        where = [jax.random.randint(jax.random.fold_in(own_key, axis), (), 0, length) for axis, length in enumerate(array.shape)]
        where[longest] = (where[longest] + shift) % array.shape[longest]
        spots.append(tuple(where))
    return array.at[spots[0]].set(low).at[spots[1]].set(largest)


def block_scale(key, dims, cuts, least, largest):
    loudness, own = 1.0, jax.random.fold_in(key, 6)
    for position, shards_of in cuts:
        heights = jnp.exp(jax.random.uniform(jax.random.fold_in(own, position), (shards_of,), jnp.float32, least / len(cuts), largest / len(cuts)))
        loudness = loudness * jnp.repeat(heights, dims[position] // shards_of).reshape([-1 if axis == position else 1 for axis in range(len(dims))])
    return loudness


def routed_block(rng, own, number, rows, number_of, top, most, slope):
    order = jax.random.permutation(rng, number_of)
    crowded, usual = shares(number_of, rows * top, most, slope, True), shares(number_of, rows * top, most, slope, False)
    places = jnp.arange(number_of)

    def named(lengths, rotation):
        used = int((lengths > 0).sum())
        fixed = max(1, used // 4)
        moved = fixed + (places - fixed + rotation * (used - fixed)) % max(1, number_of - fixed)
        return jnp.zeros((number_of,), jnp.int32).at[order[jnp.where(places < fixed, places, moved)]].set(jnp.asarray(lengths, jnp.int32))

    lengths = jnp.where(number % 4 == 0, named(crowded, number // 4), named(usual, number - number // 4 - 1))
    mixed = jax.random.permutation(jax.random.fold_in(own, 3), number_of)
    giver, receiver = mixed[0:number_of // 2 * 2:2], mixed[1:number_of // 2 * 2:2]
    margin = jnp.minimum(lengths[giver] - 1, most - lengths[receiver]) // 2
    margin = jnp.where((giver == order[0]) | (receiver == order[0]) | (lengths[receiver] == 0), 0, jnp.maximum(margin, 0))
    moved = jax.random.randint(jax.random.fold_in(own, 4), (number_of // 2,), 0, 1 << 20) % (margin + 1)
    lengths = lengths.at[giver].add(-moved).at[receiver].add(moved)
    items = jnp.searchsorted(jnp.cumsum(lengths), jnp.arange(rows * top), side="right").astype(jnp.int32)
    table = items.reshape(top, rows).T
    table = table[jax.random.permutation(jax.random.fold_in(own, 1), rows)]
    rotation = jax.random.randint(jax.random.fold_in(own, 2), (rows, 1), 0, top)
    return jnp.take_along_axis(table, (jnp.arange(top)[None, :] + rotation) % top, axis=1)


def shares(count, total, bound, slope, full):
    portions = [(1 << 20) // math.isqrt(rank ** slope) + 1 for rank in range(1, count + 1)]
    largest = bound if full else min(bound, max(-(-total // count), total * portions[0] // sum(portions)))
    least = 1 if total - largest >= count - 1 else 0
    holding, spare = [largest] + [least] * (count - 1), total - largest - least * (count - 1)
    while spare > 0:
        candidates = [i for i in range(1, count) if holding[i] < largest] or [i for i in range(1, count) if holding[i] < bound]
        whole, remaining = sum([portions[i] for i in candidates]), spare
        for i in candidates:
            more = min(bound - holding[i], max(1, remaining * portions[i] // whole), spare)
            holding[i] = holding[i] + more
            spare = spare - more
    return np.array(holding)


def normal_values(own_key, shape, width, bound, cuts=(), kind=jnp.bfloat16):
    entries = width * jax.random.normal(own_key, shape, jnp.float32)
    if cuts:
        entries = entries * block_scale(own_key, shape, cuts, -0.22, 0.18)
    return jnp.clip(entries, -bound, bound).astype(kind)


def setup_inputs(seed: int = 0) -> dict:
    key_of = jax.random.split(jax.random.key(seed), 5)
    features = normal_values(key_of[0], (EXAMPLES, F), 1.0, 6.0, ((0, 32),), jnp.float32)
    sign_bits = with_ends(jax.random.randint(key_of[1], (EXAMPLES,), 0, 2), jax.random.fold_in(key_of[1], 1), 0, 1).astype(jnp.int32)
    sample_device_keys = jax.random.split(jax.random.fold_in(key_of[2], 1), SAMPLES // K_DEV)
    sample_device_turns = jax.random.permutation(jax.random.fold_in(key_of[2], 3), SAMPLES // K_DEV)
    sample_device = jax.vmap(lambda own, number: routed_block(jax.random.fold_in(key_of[2], 2), own, number, K_DEV, DEVICES, 1, MOST, 2))(sample_device_keys, sample_device_turns).reshape((SAMPLES, 1))
    sample_offset = draw_sample_offset(jax.random.fold_in(key_of[4], 71), 0)
    return {"features": features, "sign_bits": sign_bits, "sample_device": sample_device, "sample_offset": sample_offset}


def hadamard_table(order_size):
    index = jnp.arange(order_size, dtype=jnp.int32)
    common = index[:, None] & index[None, :]
    parity = jnp.zeros((order_size, order_size), jnp.int32)
    for bit_pos in range(max(order_size.bit_length(), 1)):
        parity = parity + (common >> bit_pos & 1)
    return (1 - 2 * (parity % 2)).astype(jnp.float32)

def reference(features, sign_bits, sample_device, sample_offset):
    highest = lax.Precision.HIGHEST
    sign_values = (2 * sign_bits - 1).astype(jnp.float32)
    signed = features * sign_values[:, None]
    blocks = L_DEV // 128
    grid = signed.reshape(N_EXA, N_EXB, blocks, 128, F)
    grid = jnp.einsum('ka,abcdf->kbcdf', hadamard_table(N_EXA), grid, precision=highest)
    grid = jnp.einsum('kb,abcdf->akcdf', hadamard_table(N_EXB), grid, precision=highest)
    grid = jnp.einsum('kc,abcdf->abkdf', hadamard_table(blocks), grid, precision=highest)
    grid = jnp.einsum('kd,abcdf->abckf', hadamard_table(128), grid, precision=highest)
    transformed = grid.reshape(EXAMPLES, F) / math.sqrt(EXAMPLES)
    row_index = (sample_device[:, 0] * L_DEV + sample_offset).astype(jnp.int32)
    sketch = jnp.take(transformed, row_index, axis=0)
    gram = jnp.dot(sketch.T, sketch, precision=highest) / SAMPLES
    upper_factor = jnp.linalg.cholesky(gram).T
    q_rows = lax.linalg.triangular_solve(upper_factor, sketch, left_side=False, lower=False, transpose_a=False)
    return (q_rows, upper_factor)
```

```python
import functools
import math

import jax
import jax.numpy as jnp
from jax import lax
from jax.experimental import pallas as pl
from jax.experimental.pallas import tpu as pltpu
from jax.sharding import PartitionSpec as P

F32 = jnp.float32
BF16 = jnp.bfloat16
I32 = jnp.int32
SUB = 8
MIB = 1 << 20


def parity(bits, width):
    total = jnp.zeros_like(bits)
    for place in range(width):
        total = total ^ (bits >> place)
    return total & 1


def split3(x):
    high = x.astype(BF16).astype(F32)
    rest = x - high
    mid = rest.astype(BF16).astype(F32)
    return high, mid, rest - mid


def bit_perm(size, bit):
    return [(i, i ^ bit) for i in range(size)]


def mix_low(x_ref, sign_ref, mid_ref, table):
    low = table.shape[0]
    blocks = x_ref.shape[0] // low

    def one(b, carry):
        rows = pl.ds(pl.multiple_of(b * low, low), low)
        sign = (2 * sign_ref[pl.ds(b, 1), :] - 1).astype(F32)
        left = (table * sign).astype(BF16)
        x = x_ref[rows, :]
        high = x.astype(BF16)
        rest = x - high.astype(F32)
        mid = rest.astype(BF16)
        last = (rest - mid.astype(F32)).astype(BF16)
        wide = jnp.dot(left, jnp.concatenate([high, mid], 1), preferred_element_type=F32)
        width = x.shape[1]
        tail = jnp.dot(left, last, preferred_element_type=F32)
        mid_ref[rows, :] = wide[:, :width] + (wide[:, width:] + tail)
        return carry

    lax.fori_loop(0, blocks, one, 0)


def low_table(low):
    width = max(low.bit_length() - 1, 1)
    r = lax.broadcasted_iota(I32, (low, low), 0)
    c = lax.broadcasted_iota(I32, (low, low), 1)
    return (1 - 2 * parity(r & c, width)).astype(F32)


def mix_high(mid_ref, low, emit):
    blocks = mid_ref.shape[0] // low

    def one(g, carry):
        start = pl.multiple_of(g * SUB, SUB)
        parts = [mid_ref[pl.ds(b * low + start, SUB), :] for b in range(blocks)]
        step = 1
        while step < blocks:
            mixed = list(parts)
            for b in range(blocks):
                if not b & step:
                    mixed[b] = parts[b] + parts[b | step]
                    mixed[b | step] = parts[b] - parts[b | step]
            parts = mixed
            step *= 2
        for b in range(blocks):
            emit(b * low + start, parts[b])
        return carry

    lax.fori_loop(0, low // SUB, one, 0)


def own_kernel(low, x_ref, sign_ref, out_ref, mid_ref):
    mix_low(x_ref, sign_ref, mid_ref, low_table(low))

    def emit(row, value):
        out_ref[pl.ds(row, SUB), :] = value

    mix_high(mid_ref, low, emit)


def pair_kernel(low, x_ref, sign_ref, own_ref, out_ref, mid_ref):
    mix_low(x_ref, sign_ref, mid_ref, low_table(low))
    count = x_ref.shape[0]

    def emit(row, value):
        own = own_ref[pl.ds(row, SUB), :]
        out_ref[pl.ds(row, SUB), :] = own + value
        out_ref[pl.ds(count + row, SUB), :] = own - value

    mix_high(mid_ref, low, emit)


def pick_kernel(unroll, row_ref, sign_ref, table_ref, out_ref):
    def some(i, carry):
        for u in range(unroll):
            r = i * unroll + u
            out_ref[pl.ds(r, 1), :] = table_ref[pl.ds(row_ref[r], 1), :] * sign_ref[r]
        return carry

    lax.fori_loop(0, out_ref.shape[0] // unroll, some, 0)


def pick(rows, signs, table):
    count = rows.shape[0]
    vmem = pl.BlockSpec(memory_space=pltpu.VMEM)
    smem = pl.BlockSpec(memory_space=pltpu.SMEM)
    return pl.pallas_call(
        functools.partial(pick_kernel, math.gcd(count, 32)),
        out_shape=jax.ShapeDtypeStruct((count, table.shape[1]), F32),
        in_specs=[smem, smem, vmem],
        out_specs=vmem,
        compiler_params=pltpu.CompilerParams(vmem_limit_bytes=24 * MIB),
        cost_estimate=pl.CostEstimate(
            flops=count * 128, bytes_accessed=4 * 4 * MIB, transcendentals=0
        ),
        name="pick",
    )(rows, signs, table)


def factor_panel(left, right, at):
    shape = left.shape
    rows = lax.broadcasted_iota(I32, shape, 0)
    column = [jnp.broadcast_to(left[:, at + i : at + i + 1], shape) for i in range(SUB)]
    pivots = jnp.ones_like(left)
    for i in range(SUB):
        pivot = jnp.broadcast_to(column[i][i : i + 1, :], shape)
        pivots = jnp.where(rows == i, pivot, pivots)
        if i < SUB - 1:
            ratio = jnp.where(rows > i, column[i] * (1.0 / pivot), 0.0)
            for j in range(i + 1, SUB):
                column[j] = column[j] - ratio * jnp.broadcast_to(column[j][i : i + 1, :], shape)
            left = left - ratio * jnp.broadcast_to(left[i : i + 1, :], shape)
            right = right - ratio * jnp.broadcast_to(right[i : i + 1, :], shape)
    scale = lax.rsqrt(pivots)
    return left * scale, right * scale


def factor(gram):
    n = gram.shape[0]
    rest = gram
    unit = (
        lax.broadcasted_iota(I32, (n, n), 0) == lax.broadcasted_iota(I32, (n, n), 1)
    ).astype(F32)
    lanes = lax.broadcasted_iota(I32, (SUB, n), 1)
    panel_rows = lax.broadcasted_iota(I32, (SUB, n), 0)
    uppers, inverses = [], []
    for at in range(0, n, SUB):
        left, right = factor_panel(rest[:SUB], unit[:SUB], at)
        left = jnp.where(lanes >= panel_rows + at, left, 0.0)
        uppers.append(left)
        inverses.append(right)
        if at + SUB < n:
            h, m, l = split3(left)
            uh, um, ul = split3(right)
            terms = jnp.concatenate([h, h, m, h, l, m], 0)
            others = jnp.concatenate(
                [
                    jnp.concatenate([h, m, h, l, h, m], 0),
                    jnp.concatenate([uh, um, uh, ul, uh, um], 0),
                ],
                1,
            )
            change = jnp.dot(terms.T[at + SUB :], others, preferred_element_type=F32)
            rest = rest[SUB:] - change[:, :n]
            unit = unit[SUB:] - change[:, n:]
    return jnp.concatenate(uppers, 0), jnp.concatenate(inverses, 0)


def finish_kernel(gram_ref, sketch_ref, q_ref, upper_ref):
    upper, inverse = factor(gram_ref[...])
    upper_ref[...] = upper
    q_ref[...] = lax.dot_general(
        sketch_ref[...],
        inverse,
        (((1,), (1,)), ((), ())),
        precision=lax.Precision.HIGHEST,
        preferred_element_type=F32,
    )


def per_device(features, sign_bits, sample_device, sample_offset):
    rows_dev, width = features.shape
    n_outer = lax.axis_size("exa")
    n_inner = lax.axis_size("exb")
    n_all = n_outer * n_inner
    bits = n_all.bit_length() - 1
    inner_bits = n_inner.bit_length() - 1
    myself = lax.axis_index("exa") * n_inner + lax.axis_index("exb")
    total = sample_offset.shape[0]
    own_count = total // n_all
    low = min(256, rows_dev)
    vmem = pl.BlockSpec(memory_space=pltpu.VMEM)

    def swap(value, bit):
        if bit < inner_bits:
            return lax.ppermute(value, "exb", bit_perm(n_inner, 1 << bit))
        return lax.ppermute(value, "exa", bit_perm(n_outer, 1 << (bit - inner_bits)))

    source = sample_device[:, 0]
    scale = 1.0 / math.sqrt(rows_dev * n_all)
    row_all = sample_offset + (source & 1) * rows_dev
    sign_all = (1 - 2 * parity(source & myself, bits)).astype(F32) * scale
    row_blocks = row_all.reshape(n_all, own_count)
    sign_blocks = sign_all.reshape(n_all, own_count)

    far_features = swap(features, 0)
    far_signs = swap(sign_bits, 0)
    table_shape = (rows_dev // low, low)
    half = jax.ShapeDtypeStruct((rows_dev, width), F32)
    params = pltpu.CompilerParams(vmem_limit_bytes=32 * MIB)
    scratch = [pltpu.VMEM((rows_dev, width), F32)]
    own = pl.pallas_call(
        functools.partial(own_kernel, low),
        out_shape=half,
        in_specs=[vmem, vmem],
        out_specs=vmem,
        scratch_shapes=scratch,
        compiler_params=params,
        cost_estimate=pl.CostEstimate(flops=4 * 10**9, bytes_accessed=8 * MIB, transcendentals=0),
        name="own",
    )(features, sign_bits.reshape(table_shape))
    table = pl.pallas_call(
        functools.partial(pair_kernel, low),
        out_shape=jax.ShapeDtypeStruct((2 * rows_dev, width), F32),
        in_specs=[vmem, vmem, vmem],
        out_specs=vmem,
        scratch_shapes=scratch,
        compiler_params=params,
        cost_estimate=pl.CostEstimate(flops=4 * 10**9, bytes_accessed=16 * MIB, transcendentals=0),
        name="pair",
    )(far_features, far_signs.reshape(table_shape), own)

    outer_order = list(range(inner_bits, bits))
    inner_order = list(range(1, inner_bits))
    chunk_rows = own_count // 2
    chunks = [
        (0, chunk_rows, inner_order + outer_order),
        (chunk_rows, chunk_rows, inner_order[::-1] + outer_order),
    ]

    def targets(order):
        listed = [0]
        for bit in order[::-1]:
            listed = [e | 1 << bit for e in listed] + listed
        return listed

    def take(start, count, which):
        blocks = myself ^ jnp.array(which, I32)
        rows = jnp.take(row_blocks[:, start : start + count], blocks, axis=0).reshape(-1)
        signs = jnp.take(sign_blocks[:, start : start + count], blocks, axis=0).reshape(-1)
        return pick(rows, signs, table)

    lists = [targets(order) for _, _, order in chunks]
    sent = []
    for (start, count, order), listed in zip(chunks, lists):
        send = take(start, count, listed[: len(listed) // 2])
        sent.append(swap(send, order[0]))
    kept = [take(s, c, listed[len(listed) // 2 :]) for (s, c, _), listed in zip(chunks, lists)]
    for stage in range(1, len(chunks[0][2]) + 1):
        for n, (_, _, order) in enumerate(chunks):
            sums = kept[n] + sent[n]
            if stage < len(order):
                halfway = sums.shape[0] // 2
                sent[n] = swap(sums[:halfway], order[stage])
                kept[n] = sums[halfway:]
            else:
                kept[n] = sums
    sketch = jnp.concatenate(kept, 0)

    gram = lax.dot_general(
        sketch,
        sketch,
        (((0,), (0,)), ((), ())),
        precision=lax.Precision.HIGHEST,
        preferred_element_type=F32,
    ) / total
    for bit in range(bits):
        gram = gram + swap(gram, bit)

    return pl.pallas_call(
        finish_kernel,
        out_shape=(
            jax.ShapeDtypeStruct((own_count, width), F32),
            jax.ShapeDtypeStruct((width, width), F32),
        ),
        in_specs=[vmem, vmem],
        out_specs=(vmem, vmem),
        name="finish",
    )(gram, sketch)


def solution(mesh):
    placed = (P(("exa", "exb"), None), P(("exa", "exb")), P(), P())
    return jax.shard_map(
        per_device,
        mesh=mesh,
        in_specs=placed,
        out_specs=(P(("exa", "exb"), None), P()),
        check_vma=False,
    )
```

```python
import functools
import math

import jax
import jax.numpy as jnp
from jax import lax
from jax.experimental import pallas as pl
from jax.experimental.pallas import tpu as pltpu
from jax.sharding import PartitionSpec as P

F32 = jnp.float32
BF16 = jnp.bfloat16
I32 = jnp.int32
SUB = 8
PER_WORD = 32
GROUP = SUB * PER_WORD
BLOCK = 4 * GROUP
MIB = 1 << 20


def parity(bits, width):
    total = jnp.zeros_like(bits)
    for place in range(width):
        total = total ^ (bits >> place)
    return total & 1


def split3(x):
    high = x.astype(BF16).astype(F32)
    rest = x - high
    mid = rest.astype(BF16).astype(F32)
    return high, mid, rest - mid


def bit_perm(size, bit):
    return [(i, i ^ bit) for i in range(size)]


def butterfly(parts, steps):
    for step in steps:
        mixed = list(parts)
        for i in range(len(parts)):
            if not i & step:
                mixed[i] = parts[i] + parts[i | step]
                mixed[i | step] = parts[i] - parts[i | step]
        parts = mixed
    return parts


def powers(count):
    return [1 << i for i in range(count.bit_length() - 1)]


def word_bit(v):
    return 1 << v if v < 31 else -(1 << 31)


def mix_block(x_ref, word_ref, out_ref, at):
    def signed_group(g, carry):
        base = pl.multiple_of(at + g * GROUP, GROUP)
        words = word_ref[pl.ds(pl.multiple_of(base // PER_WORD, SUB), SUB), :]
        parts = []
        for v in range(PER_WORD):
            part = x_ref[pl.ds(base + SUB * v, SUB), :]
            parts.append(jnp.where((words & word_bit(v)) != 0, part, -part))
        for v, part in enumerate(butterfly(parts, powers(PER_WORD))):
            out_ref[pl.ds(base + SUB * v, SUB), :] = part
        return carry

    lax.fori_loop(0, BLOCK // GROUP, signed_group, 0)

    def within_group(m, carry):
        base = pl.multiple_of(at + m * SUB * SUB, SUB * SUB)
        spots = [GROUP * k for k in range(BLOCK // GROUP)]
        parts = [
            out_ref[pl.ds(base + spot + t, SUB, stride=SUB), :] for spot in spots for t in range(SUB)
        ]
        parts = butterfly(parts, powers(len(parts)))
        for k, spot in enumerate(spots):
            for t in range(SUB):
                out_ref[pl.ds(base + spot + SUB * t, SUB), :] = parts[SUB * k + t]
        return carry

    lax.fori_loop(0, GROUP // (SUB * SUB), within_group, 0)


def spread_signs(bits_ref, word_ref):
    lanes = bits_ref.shape[1]
    at = lax.broadcasted_iota(I32, (SUB, lanes), 1)
    row = lax.broadcasted_iota(I32, (SUB, lanes), 0)
    weights = jnp.where(at % SUB == row, 1 << (at // SUB), 0).astype(F32)
    halves = lax.dot_general(
        weights, bits_ref[...].astype(F32), (((1,), (1,)), ((), ())), preferred_element_type=F32
    ).astype(I32)
    for g in range(word_ref.shape[0] // SUB):
        word = halves[:, 2 * g : 2 * g + 1] | halves[:, 2 * g + 1 : 2 * g + 2] << (lanes // SUB)
        word_ref[SUB * g : SUB * g + SUB, :] = jnp.broadcast_to(word, (SUB, word_ref.shape[1]))


def table_row(row):
    return (row & ~63) | ((row & 7) << 3) | ((row >> 3) & 7)


def mix_blocks(x_ref, bits_ref, x, mid, word_ref, sems, emit):
    blocks = mid.shape[0] // BLOCK

    def fetch(h):
        rows = pl.ds(pl.multiple_of(h * BLOCK, BLOCK), BLOCK)
        return pltpu.make_async_copy(x_ref.at[rows], x.at[rows], sems.at[h])

    for h in range(blocks):
        fetch(h).start()
    spread_signs(bits_ref, word_ref)

    def one(h, carry):
        fetch(h).wait()
        mix_block(x, word_ref, mid, h * BLOCK)
        return carry

    lax.fori_loop(0, blocks, one, 0)

    def across(g, carry):
        row = pl.multiple_of(g * SUB, SUB)
        parts = [mid[pl.ds(BLOCK * h + row, SUB), :] for h in range(blocks)]
        for h, part in enumerate(butterfly(parts, powers(blocks))):
            emit(BLOCK * h + row, part)
        return carry

    lax.fori_loop(0, BLOCK // SUB, across, 0, unroll=4)


def own_kernel(
    scale, spans, x_ref, bits_ref, me_ref, source_ref, offset_ref, out_ref, *refs
):
    x, mid, words, sems = refs[-4:]
    rows_dev = x.shape[0]
    me = me_ref[0]
    for n, span in enumerate(spans):
        row_ref, sign_ref = refs[2 * n], refs[2 * n + 1]
        to = 0
        for target, block, start, count in span:
            at = pl.multiple_of((me ^ target) * block + start, math.gcd(128, start, count))
            source = source_ref[:, pl.ds(at, count)]
            offset = offset_ref[:, pl.ds(at, count)]
            row_ref[:, to : to + count] = table_row(offset) + (source & 1) * rows_dev
            odd = parity(source & me, 16) != 0
            sign_ref[:, to : to + count] = jnp.where(odd, -scale, scale)
            to += count

    def emit(row, value):
        out_ref[pl.ds(row, SUB), :] = value

    mix_blocks(x_ref, bits_ref, x, mid, words, sems, emit)


def pair_kernel(x_ref, bits_ref, own_ref, out_ref, x, mid, words, sems):
    count = x.shape[0]

    def emit(row, value):
        own = own_ref[pl.ds(row, SUB), :]
        out_ref[pl.ds(row, SUB), :] = own + value
        out_ref[pl.ds(count + row, SUB), :] = own - value

    mix_blocks(x_ref, bits_ref, x, mid, words, sems, emit)


def pick_kernel(row_ref, sign_ref, table_ref, out_ref):
    count = out_ref.shape[0]
    unroll = math.gcd(count, 32)

    def some(i, carry):
        for u in range(unroll):
            r = i * unroll + u
            out_ref[pl.ds(r, 1), :] = table_ref[pl.ds(row_ref[0, r], 1), :] * sign_ref[0, r]
        return carry

    lax.fori_loop(0, count // unroll, some, 0)


def pick(places, table):
    rows, signs = places
    count = rows.shape[1]
    vmem = pl.BlockSpec(memory_space=pltpu.VMEM)
    smem = pl.BlockSpec(memory_space=pltpu.SMEM)
    return pl.pallas_call(
        pick_kernel,
        out_shape=jax.ShapeDtypeStruct((count, table.shape[1]), F32),
        in_specs=[smem, smem, vmem],
        out_specs=vmem,
        compiler_params=pltpu.CompilerParams(vmem_limit_bytes=14 * MIB),
        cost_estimate=pl.CostEstimate(
            flops=count * 128, bytes_accessed=count * 6 * 1024, transcendentals=0
        ),
        name="pick",
    )(rows, signs, pltpu.with_memory_space_constraint(table, pltpu.VMEM))


def factor_panel(left, right, at):
    shape = left.shape
    rows = lax.broadcasted_iota(I32, shape, 0)
    column = [jnp.broadcast_to(left[:, at + i : at + i + 1], shape) for i in range(SUB)]
    pivots = jnp.ones_like(left)
    for i in range(SUB):
        pivot = jnp.broadcast_to(column[i][i : i + 1, :], shape)
        pivots = jnp.where(rows == i, pivot, pivots)
        if i < SUB - 1:
            ratio = jnp.where(rows > i, column[i] * (1.0 / pivot), 0.0)
            for j in range(i + 1, SUB):
                column[j] = column[j] - ratio * jnp.broadcast_to(column[j][i : i + 1, :], shape)
            left = left - ratio * jnp.broadcast_to(left[i : i + 1, :], shape)
            right = right - ratio * jnp.broadcast_to(right[i : i + 1, :], shape)
    scale = lax.rsqrt(pivots)
    return left * scale, right * scale


def factor(gram):
    n = gram.shape[0]
    rest = gram
    unit = (
        lax.broadcasted_iota(I32, (n, n), 0) == lax.broadcasted_iota(I32, (n, n), 1)
    ).astype(F32)
    lanes = lax.broadcasted_iota(I32, (SUB, n), 1)
    panel_rows = lax.broadcasted_iota(I32, (SUB, n), 0)
    uppers, inverses = [], []
    for at in range(0, n, SUB):
        left, right = factor_panel(rest[:SUB], unit[:SUB], at)
        left = jnp.where(lanes >= panel_rows + at, left, 0.0)
        uppers.append(left)
        inverses.append(right)
        if at + SUB < n:
            h, m, l = split3(left)
            uh, um, ul = split3(right)
            terms = jnp.concatenate([h, h, m, h, l, m], 0)
            others = jnp.concatenate(
                [
                    jnp.concatenate([h, m, h, l, h, m], 0),
                    jnp.concatenate([uh, um, uh, ul, uh, um], 0),
                ],
                1,
            )
            change = jnp.dot(terms.T[at + SUB :], others, preferred_element_type=F32)
            rest = rest[SUB:] - change[:, :n]
            unit = unit[SUB:] - change[:, n:]
    return jnp.concatenate(uppers, 0), jnp.concatenate(inverses, 0)


def finish_kernel(gram_ref, sketch_ref, q_ref, upper_ref):
    upper, inverse = factor(gram_ref[...])
    upper_ref[...] = upper
    q_ref[...] = lax.dot_general(
        sketch_ref[...],
        inverse,
        (((1,), (1,)), ((), ())),
        precision=lax.Precision.HIGHEST,
        preferred_element_type=F32,
    )


def per_device(features, sign_bits, sample_device, sample_offset):
    rows_dev, width = features.shape
    n_outer = lax.axis_size("exa")
    n_inner = lax.axis_size("exb")
    n_all = n_outer * n_inner
    bits = n_all.bit_length() - 1
    inner_bits = n_inner.bit_length() - 1
    myself = lax.axis_index("exa") * n_inner + lax.axis_index("exb")
    total = sample_offset.shape[0]
    own_count = total // n_all
    vmem = pl.BlockSpec(memory_space=pltpu.VMEM)

    def swap(value, mask):
        if mask < n_inner:
            return lax.ppermute(value, "exb", bit_perm(n_inner, mask))
        return lax.ppermute(value, "exa", bit_perm(n_outer, mask // n_inner))

    outer = tuple(range(inner_bits, bits))
    inner = [(bit,) for bit in range(1, inner_bits)]
    chunk_rows = own_count // 2
    chunks = [
        (0, chunk_rows, inner + [outer]),
        (chunk_rows, chunk_rows, inner[::-1] + [outer]),
    ]

    def masks(step):
        listed = [0]
        for bit in step:
            listed = [e | 1 << bit for e in listed] + listed
        return listed

    def targets(steps):
        listed = [0]
        for step in steps[::-1]:
            listed = [m | e for m in masks(step) for e in listed]
        return listed

    firsts = []
    for start, count, steps in chunks:
        listed = targets(steps)
        moves = masks(steps[0])
        per = len(listed) // len(moves)
        firsts.append(
            [
                [(e, own_count, start, count) for e in listed[i * per : i * per + per]]
                for i in range(len(moves))
            ]
        )
    flat = [piece for pieces in firsts for piece in pieces]

    far_features = swap(features, 1)
    far_signs = swap(sign_bits, 1)
    params = pltpu.CompilerParams(vmem_limit_bytes=22 * MIB)
    scratch = [
        pltpu.VMEM((rows_dev, width), F32),
        pltpu.VMEM((rows_dev, width), F32),
        pltpu.VMEM((rows_dev // PER_WORD, width), I32),
        pltpu.SemaphoreType.DMA((rows_dev // BLOCK,)),
    ]
    bits_shape = (rows_dev // 128, 128)
    place_shapes = [
        jax.ShapeDtypeStruct((1, sum(count for _, _, _, count in piece)), kind)
        for piece in flat
        for kind in (I32, F32)
    ]
    own, *places = pl.pallas_call(
        functools.partial(own_kernel, 1.0 / math.sqrt(rows_dev * n_all), flat),
        out_shape=[jax.ShapeDtypeStruct((rows_dev, width), F32)] + place_shapes,
        in_specs=[
            pl.BlockSpec(memory_space=pl.ANY),
            vmem,
            pl.BlockSpec(memory_space=pltpu.SMEM),
            vmem,
            vmem,
        ],
        out_specs=[vmem] * (1 + len(place_shapes)),
        scratch_shapes=scratch,
        compiler_params=params,
        cost_estimate=pl.CostEstimate(flops=10**7, bytes_accessed=12 * MIB, transcendentals=0),
        name="own",
    )(
        pltpu.with_memory_space_constraint(features, pltpu.HBM),
        sign_bits.reshape(bits_shape),
        myself.reshape(1),
        sample_device.reshape(1, total),
        sample_offset.reshape(1, total),
    )
    table = pl.pallas_call(
        pair_kernel,
        out_shape=jax.ShapeDtypeStruct((2 * rows_dev, width), F32),
        in_specs=[pl.BlockSpec(memory_space=pl.ANY), vmem, vmem],
        out_specs=vmem,
        scratch_shapes=scratch,
        compiler_params=params,
        cost_estimate=pl.CostEstimate(flops=10**7, bytes_accessed=16 * MIB, transcendentals=0),
        name="pair",
    )(
        far_features,
        far_signs.reshape(bits_shape),
        pltpu.with_memory_space_constraint(own, pltpu.VMEM),
    )

    pairs = iter(zip(places[::2], places[1::2]))
    mine = [[next(pairs) for _ in pieces] for pieces in firsts]
    sent = [
        [swap(pick(one, table), mask) for one, mask in zip(some[:-1], masks(steps[0]))]
        for some, (_, _, steps) in zip(mine, chunks)
    ]
    kept = [pick(some[-1], table) for some in mine]
    for turn in range(1, max(len(steps) for _, _, steps in chunks) + 1):
        for n, (_, _, steps) in enumerate(chunks):
            if turn > len(steps):
                continue
            sums = functools.reduce(jnp.add, sent[n], kept[n])
            if turn < len(steps):
                listed = masks(steps[turn])
                per = sums.shape[0] // len(listed)
                sent[n] = [
                    swap(sums[i * per : i * per + per], move) for i, move in enumerate(listed[:-1])
                ]
                sums = sums[-per:]
            kept[n] = sums
    sketch = jnp.concatenate(kept, 0)

    gram = lax.dot_general(
        sketch,
        sketch,
        (((0,), (0,)), ((), ())),
        precision=lax.Precision.HIGHEST,
        preferred_element_type=F32,
    ) / total
    for bit in range(bits):
        gram = gram + swap(gram, 1 << bit)

    return pl.pallas_call(
        finish_kernel,
        out_shape=(
            jax.ShapeDtypeStruct((own_count, width), F32),
            jax.ShapeDtypeStruct((width, width), F32),
        ),
        in_specs=[vmem, vmem],
        out_specs=(vmem, vmem),
        name="finish",
    )(gram, sketch)


def solution(mesh):
    placed = (P(("exa", "exb"), None), P(("exa", "exb")), P(), P())
    return jax.shard_map(
        per_device,
        mesh=mesh,
        in_specs=placed,
        out_specs=(P(("exa", "exb"), None), P()),
        check_vma=False,
    )
```

```python
import functools
import math

import jax
import jax.numpy as jnp
from jax import lax
from jax.experimental import pallas as pl
from jax.experimental.pallas import tpu as pltpu
from jax.sharding import PartitionSpec as P

F32 = jnp.float32
BF16 = jnp.bfloat16
I32 = jnp.int32
SUB = 8
PER_WORD = 32
GROUP = SUB * PER_WORD
BLOCK = 4 * GROUP
MIB = 1 << 20


def parity(bits, width):
    total = jnp.zeros_like(bits)
    for place in range(width):
        total = total ^ (bits >> place)
    return total & 1


def split3(x):
    high = x.astype(BF16).astype(F32)
    rest = x - high
    mid = rest.astype(BF16).astype(F32)
    return high, mid, rest - mid


def bit_perm(size, bit):
    return [(i, i ^ bit) for i in range(size)]


def butterfly(parts, steps):
    for step in steps:
        mixed = list(parts)
        for i in range(len(parts)):
            if not i & step:
                mixed[i] = parts[i] + parts[i | step]
                mixed[i | step] = parts[i] - parts[i | step]
        parts = mixed
    return parts


def powers(count):
    return [1 << i for i in range(count.bit_length() - 1)]


def word_bit(v):
    return 1 << v if v < 31 else -(1 << 31)


def mix_block(x_ref, word_ref, out_ref, at):
    def signed_group(g, carry):
        base = pl.multiple_of(at + g * GROUP, GROUP)
        words = word_ref[pl.ds(pl.multiple_of(base // PER_WORD, SUB), SUB), :]
        parts = []
        for v in range(PER_WORD):
            part = x_ref[pl.ds(base + SUB * v, SUB), :]
            parts.append(jnp.where((words & word_bit(v)) != 0, part, -part))
        for v, part in enumerate(butterfly(parts, powers(PER_WORD))):
            out_ref[pl.ds(base + SUB * v, SUB), :] = part
        return carry

    lax.fori_loop(0, BLOCK // GROUP, signed_group, 0)

    def within_group(m, carry):
        base = pl.multiple_of(at + m * SUB * SUB, SUB * SUB)
        spots = [GROUP * k for k in range(BLOCK // GROUP)]
        parts = [
            out_ref[pl.ds(base + spot + t, SUB, stride=SUB), :] for spot in spots for t in range(SUB)
        ]
        parts = butterfly(parts, powers(len(parts)))
        for k, spot in enumerate(spots):
            for t in range(SUB):
                out_ref[pl.ds(base + spot + SUB * t, SUB), :] = parts[SUB * k + t]
        return carry

    lax.fori_loop(0, GROUP // (SUB * SUB), within_group, 0)


def spread_signs(bits_ref, word_ref):
    lanes = bits_ref.shape[1]
    at = lax.broadcasted_iota(I32, (SUB, lanes), 1)
    row = lax.broadcasted_iota(I32, (SUB, lanes), 0)
    weights = jnp.where(at % SUB == row, 1 << (at // SUB), 0).astype(F32)
    halves = lax.dot_general(
        weights, bits_ref[...].astype(F32), (((1,), (1,)), ((), ())), preferred_element_type=F32
    ).astype(I32)
    for g in range(word_ref.shape[0] // SUB):
        word = halves[:, 2 * g : 2 * g + 1] | halves[:, 2 * g + 1 : 2 * g + 2] << (lanes // SUB)
        word_ref[SUB * g : SUB * g + SUB, :] = jnp.broadcast_to(word, (SUB, word_ref.shape[1]))


def table_row(row):
    return (row & ~63) | ((row & 7) << 3) | ((row >> 3) & 7)


def mix_blocks(x_ref, bits_ref, x, mid, word_ref, sems, emit):
    blocks = mid.shape[0] // BLOCK

    def fetch(h):
        rows = pl.ds(pl.multiple_of(h * BLOCK, BLOCK), BLOCK)
        return pltpu.make_async_copy(x_ref.at[rows], x.at[rows], sems.at[h])

    for h in range(blocks):
        fetch(h).start()
    spread_signs(bits_ref, word_ref)

    def one(h, carry):
        fetch(h).wait()
        mix_block(x, word_ref, mid, h * BLOCK)
        return carry

    lax.fori_loop(0, blocks, one, 0)

    def across(g, carry):
        row = pl.multiple_of(g * SUB, SUB)
        parts = [mid[pl.ds(BLOCK * h + row, SUB), :] for h in range(blocks)]
        for h, part in enumerate(butterfly(parts, powers(blocks))):
            emit(BLOCK * h + row, part)
        return carry

    lax.fori_loop(0, BLOCK // SUB, across, 0, unroll=4)


def own_kernel(
    scale, targets, pieces, x_ref, bits_ref, me_ref, source_ref, offset_ref, out_ref, *refs
):
    x, mid, words, sems = refs[-4:]
    rows_dev = x.shape[0]
    me = me_ref[0]
    block = source_ref.shape[1] // targets
    for target in range(0, targets, 2):
        at = pl.multiple_of((me ^ target) * block, math.gcd(128, block))
        source = source_ref[:, pl.ds(at, block)]
        rows = table_row(offset_ref[:, pl.ds(at, block)]) + (source & 1) * rows_dev
        signs = jnp.where(parity(source & me, 16) != 0, -scale, scale)
        for n, (which, start, count) in enumerate(pieces):
            if target in which:
                to = which.index(target) * count
                refs[2 * n][:, to : to + count] = rows[:, start : start + count]
                refs[2 * n + 1][:, to : to + count] = signs[:, start : start + count]

    def emit(row, value):
        out_ref[pl.ds(row, SUB), :] = value

    mix_blocks(x_ref, bits_ref, x, mid, words, sems, emit)


def pair_kernel(x_ref, bits_ref, own_ref, out_ref, x, mid, words, sems):
    count = x.shape[0]

    def emit(row, value):
        own = own_ref[pl.ds(row, SUB), :]
        out_ref[pl.ds(row, SUB), :] = own + value
        out_ref[pl.ds(count + row, SUB), :] = own - value

    mix_blocks(x_ref, bits_ref, x, mid, words, sems, emit)


def pick_kernel(row_ref, sign_ref, table_ref, *refs):
    out_ref = refs[-1]
    count = out_ref.shape[0]
    unroll = math.gcd(count, 32)

    def some(i, carry):
        for u in range(unroll):
            r = i * unroll + u
            out_ref[pl.ds(r, 1), :] = table_ref[pl.ds(row_ref[0, r], 1), :] * sign_ref[0, r]
        return carry

    lax.fori_loop(0, count // unroll, some, 0)


def pick(places, table, after=()):
    rows, signs = places
    count = rows.shape[1]
    vmem = pl.BlockSpec(memory_space=pltpu.VMEM)
    smem = pl.BlockSpec(memory_space=pltpu.SMEM)
    return pl.pallas_call(
        pick_kernel,
        out_shape=jax.ShapeDtypeStruct((count, table.shape[1]), F32),
        in_specs=[smem, smem, vmem] + [pl.BlockSpec(memory_space=pl.ANY)] * len(after),
        out_specs=vmem,
        compiler_params=pltpu.CompilerParams(vmem_limit_bytes=14 * MIB),
        cost_estimate=pl.CostEstimate(
            flops=1024, bytes_accessed=1024, transcendentals=0
        ),
        name="pick",
    )(rows, signs, pltpu.with_memory_space_constraint(table, pltpu.VMEM), *after)


def factor_panel(left, right, at):
    shape = left.shape
    rows = lax.broadcasted_iota(I32, shape, 0)
    column = [jnp.broadcast_to(left[:, at + i : at + i + 1], shape) for i in range(SUB)]
    pivots = jnp.ones_like(left)
    for i in range(SUB):
        pivot = jnp.broadcast_to(column[i][i : i + 1, :], shape)
        pivots = jnp.where(rows == i, pivot, pivots)
        if i < SUB - 1:
            ratio = jnp.where(rows > i, column[i] * (1.0 / pivot), 0.0)
            for j in range(i + 1, SUB):
                column[j] = column[j] - ratio * jnp.broadcast_to(column[j][i : i + 1, :], shape)
            left = left - ratio * jnp.broadcast_to(left[i : i + 1, :], shape)
            right = right - ratio * jnp.broadcast_to(right[i : i + 1, :], shape)
    scale = lax.rsqrt(pivots)
    return left * scale, right * scale


def factor(gram):
    n = gram.shape[0]
    rest = gram
    unit = (
        lax.broadcasted_iota(I32, (n, n), 0) == lax.broadcasted_iota(I32, (n, n), 1)
    ).astype(F32)
    lanes = lax.broadcasted_iota(I32, (SUB, n), 1)
    panel_rows = lax.broadcasted_iota(I32, (SUB, n), 0)
    uppers, inverses = [], []
    for at in range(0, n, SUB):
        left, right = factor_panel(rest[:SUB], unit[:SUB], at)
        left = jnp.where(lanes >= panel_rows + at, left, 0.0)
        uppers.append(left)
        inverses.append(right)
        if at + SUB < n:
            h, m, l = split3(left)
            uh, um, ul = split3(right)
            terms = jnp.concatenate([h, h, m, h, l, m], 0)
            others = jnp.concatenate(
                [
                    jnp.concatenate([h, m, h, l, h, m], 0),
                    jnp.concatenate([uh, um, uh, ul, uh, um], 0),
                ],
                1,
            )
            change = jnp.dot(terms.T[at + SUB :], others, preferred_element_type=F32)
            rest = rest[SUB:] - change[:, :n]
            unit = unit[SUB:] - change[:, n:]
    return jnp.concatenate(uppers, 0), jnp.concatenate(inverses, 0)


def finish_kernel(gram_ref, sketch_ref, q_ref, upper_ref):
    upper, inverse = factor(gram_ref[...])
    upper_ref[...] = upper
    q_ref[...] = lax.dot_general(
        sketch_ref[...],
        inverse,
        (((1,), (1,)), ((), ())),
        precision=lax.Precision.HIGHEST,
        preferred_element_type=F32,
    )


def per_device(features, sign_bits, sample_device, sample_offset):
    rows_dev, width = features.shape
    n_outer = lax.axis_size("exa")
    n_inner = lax.axis_size("exb")
    n_all = n_outer * n_inner
    bits = n_all.bit_length() - 1
    inner_bits = n_inner.bit_length() - 1
    myself = lax.axis_index("exa") * n_inner + lax.axis_index("exb")
    total = sample_offset.shape[0]
    own_count = total // n_all
    vmem = pl.BlockSpec(memory_space=pltpu.VMEM)

    def swap(value, mask):
        if mask < n_inner:
            return lax.ppermute(value, "exb", bit_perm(n_inner, mask))
        return lax.ppermute(value, "exa", bit_perm(n_outer, mask // n_inner))

    outer = tuple(range(inner_bits, bits))
    inner = [(bit,) for bit in range(1, inner_bits)]
    back = inner[::-1]
    orders = [(16, inner[:1] + [outer[:1]] + inner[1:] + [outer[1:]]), (16, back[:1] + [outer[:1]] + back[1:] + [outer[1:]]), (16, inner + [(bit,) for bit in outer]), (16, back + [(bit,) for bit in outer])]
    chunks, start = [], 0
    for share, steps in orders:
        chunks.append((start, own_count * share // 64, steps))
        start += own_count * share // 64

    def masks(step):
        listed = [0]
        for bit in step:
            listed = [e | 1 << bit for e in listed] + listed
        return listed

    def targets(steps):
        listed = [0]
        for step in steps[::-1]:
            listed = [m | e for m in masks(step) for e in listed]
        return listed

    firsts = []
    for start, count, steps in chunks:
        listed = targets(steps)
        moves = masks(steps[0])
        per = len(listed) // len(moves)
        firsts.append(
            [
                (listed[i * per : i * per + per], start, count)
                for i in range(len(moves))
            ]
        )
    flat = [piece for pieces in firsts for piece in pieces]

    far_features = swap(features, 1)
    far_signs = swap(sign_bits, 1)
    params = pltpu.CompilerParams(vmem_limit_bytes=22 * MIB)
    scratch = [
        pltpu.VMEM((rows_dev, width), F32),
        pltpu.VMEM((rows_dev, width), F32),
        pltpu.VMEM((rows_dev // PER_WORD, width), I32),
        pltpu.SemaphoreType.DMA((rows_dev // BLOCK,)),
    ]
    bits_shape = (rows_dev // 128, 128)
    place_shapes = [
        jax.ShapeDtypeStruct((1, len(which) * count), kind)
        for which, _, count in flat
        for kind in (I32, F32)
    ]
    own, *places = pl.pallas_call(
        functools.partial(own_kernel, 1.0 / math.sqrt(rows_dev * n_all), n_all, flat),
        out_shape=[jax.ShapeDtypeStruct((rows_dev, width), F32)] + place_shapes,
        in_specs=[
            pl.BlockSpec(memory_space=pl.ANY),
            vmem,
            pl.BlockSpec(memory_space=pltpu.SMEM),
            vmem,
            vmem,
        ],
        out_specs=[vmem] * (1 + len(place_shapes)),
        scratch_shapes=scratch,
        compiler_params=params,
        cost_estimate=pl.CostEstimate(flops=10**7, bytes_accessed=12 * MIB, transcendentals=0),
        name="own",
    )(
        pltpu.with_memory_space_constraint(features, pltpu.HBM),
        sign_bits.reshape(bits_shape),
        myself.reshape(1),
        sample_device.reshape(1, total),
        sample_offset.reshape(1, total),
    )
    table = pl.pallas_call(
        pair_kernel,
        out_shape=jax.ShapeDtypeStruct((2 * rows_dev, width), F32),
        in_specs=[pl.BlockSpec(memory_space=pl.ANY), vmem, vmem],
        out_specs=vmem,
        scratch_shapes=scratch,
        compiler_params=params,
        cost_estimate=pl.CostEstimate(flops=10**7, bytes_accessed=16 * MIB, transcendentals=0),
        name="pair",
    )(
        far_features,
        far_signs.reshape(bits_shape),
        pltpu.with_memory_space_constraint(own, pltpu.VMEM),
    )

    pairs = iter(zip(places[::2], places[1::2]))
    mine = [[next(pairs) for _ in pieces] for pieces in firsts]
    sent = [
        [swap(pick(one, table), mask) for one, mask in zip(some[:-1], masks(steps[0]))]
        for some, (_, _, steps) in zip(mine, chunks)
    ]
    waits = [None,None,0,1]
    kept = [
        pick(some[-1], table, () if wait is None else (sent[wait][0],))
        for some, wait in zip(mine, waits)
    ]
    for turn in range(1, max(len(steps) for _, _, steps in chunks) + 1):
        for n, (_, _, steps) in enumerate(chunks):
            if turn > len(steps):
                continue
            sums = functools.reduce(jnp.add, sent[n], kept[n])
            if turn < len(steps):
                listed = masks(steps[turn])
                per = sums.shape[0] // len(listed)
                sent[n] = [
                    swap(sums[i * per : i * per + per], move) for i, move in enumerate(listed[:-1])
                ]
                sums = sums[-per:]
            kept[n] = sums
    sketch = jnp.concatenate(kept, 0)

    gram = lax.dot_general(
        sketch,
        sketch,
        (((0,), (0,)), ((), ())),
        precision=lax.Precision.HIGHEST,
        preferred_element_type=F32,
    ) / total
    for bit in range(bits):
        gram = gram + swap(gram, 1 << bit)

    return pl.pallas_call(
        finish_kernel,
        out_shape=(
            jax.ShapeDtypeStruct((own_count, width), F32),
            jax.ShapeDtypeStruct((width, width), F32),
        ),
        in_specs=[vmem, vmem],
        out_specs=(vmem, vmem),
        name="finish",
    )(gram, sketch)


def solution(mesh):
    placed = (P(("exa", "exb"), None), P(("exa", "exb")), P(), P())
    return jax.shard_map(
        per_device,
        mesh=mesh,
        in_specs=placed,
        out_specs=(P(("exa", "exb"), None), P()),
        check_vma=False,
    )
```

```python
import functools
import math

import jax
import jax.numpy as jnp
from jax import lax
from jax.experimental import pallas as pl
from jax.experimental.pallas import tpu as pltpu
from jax.sharding import PartitionSpec as P

F32 = jnp.float32
BF16 = jnp.bfloat16
I32 = jnp.int32
SUB = 8
PER_WORD = 32
GROUP = SUB * PER_WORD
BLOCK = 4 * GROUP
MIB = 1 << 20


def parity(bits, width):
    total = jnp.zeros_like(bits)
    for place in range(width):
        total = total ^ (bits >> place)
    return total & 1


def split3(x):
    high = x.astype(BF16).astype(F32)
    rest = x - high
    mid = rest.astype(BF16).astype(F32)
    return high, mid, rest - mid


def bit_perm(size, bit):
    return [(i, i ^ bit) for i in range(size)]


def butterfly(parts, steps):
    for step in steps:
        mixed = list(parts)
        for i in range(len(parts)):
            if not i & step:
                mixed[i] = parts[i] + parts[i | step]
                mixed[i | step] = parts[i] - parts[i | step]
        parts = mixed
    return parts


def powers(count):
    return [1 << i for i in range(count.bit_length() - 1)]


def word_bit(v):
    return 1 << v if v < 31 else -(1 << 31)


def mix_block(x_ref, word_ref, out_ref, at):
    def signed_group(g, carry):
        base = pl.multiple_of(at + g * GROUP, GROUP)
        words = word_ref[pl.ds(pl.multiple_of(base // PER_WORD, SUB), SUB), :]
        parts = []
        for v in range(PER_WORD):
            part = x_ref[pl.ds(base + SUB * v, SUB), :]
            parts.append(jnp.where((words & word_bit(v)) != 0, part, -part))
        for v, part in enumerate(butterfly(parts, powers(PER_WORD))):
            out_ref[pl.ds(base + SUB * v, SUB), :] = part
        return carry

    lax.fori_loop(0, BLOCK // GROUP, signed_group, 0)

    def within_group(m, carry):
        base = pl.multiple_of(at + m * SUB * SUB, SUB * SUB)
        spots = [GROUP * k for k in range(BLOCK // GROUP)]
        parts = [
            out_ref[pl.ds(base + spot + t, SUB, stride=SUB), :] for spot in spots for t in range(SUB)
        ]
        parts = butterfly(parts, powers(len(parts)))
        for k, spot in enumerate(spots):
            for t in range(SUB):
                out_ref[pl.ds(base + spot + SUB * t, SUB), :] = parts[SUB * k + t]
        return carry

    lax.fori_loop(0, GROUP // (SUB * SUB), within_group, 0)


def spread_signs(bits_ref, word_ref):
    lanes = bits_ref.shape[1]
    at = lax.broadcasted_iota(I32, (SUB, lanes), 1)
    row = lax.broadcasted_iota(I32, (SUB, lanes), 0)
    weights = jnp.where(at % SUB == row, 1 << (at // SUB), 0).astype(F32)
    halves = lax.dot_general(
        weights, bits_ref[...].astype(F32), (((1,), (1,)), ((), ())), preferred_element_type=F32
    ).astype(I32)
    for g in range(word_ref.shape[0] // SUB):
        word = halves[:, 2 * g : 2 * g + 1] | halves[:, 2 * g + 1 : 2 * g + 2] << (lanes // SUB)
        word_ref[SUB * g : SUB * g + SUB, :] = jnp.broadcast_to(word, (SUB, word_ref.shape[1]))


def table_row(row):
    return (row & ~63) | ((row & 7) << 3) | ((row >> 3) & 7)


def mix_blocks(x_ref, bits_ref, x, mid, word_ref, sems, emit):
    blocks = mid.shape[0] // BLOCK

    def fetch(h):
        rows = pl.ds(pl.multiple_of(h * BLOCK, BLOCK), BLOCK)
        return pltpu.make_async_copy(x_ref.at[rows], x.at[rows], sems.at[h])

    for h in range(blocks):
        fetch(h).start()
    spread_signs(bits_ref, word_ref)

    def one(h, carry):
        fetch(h).wait()
        mix_block(x, word_ref, mid, h * BLOCK)
        return carry

    lax.fori_loop(0, blocks, one, 0)

    def across(g, carry):
        row = pl.multiple_of(g * SUB, SUB)
        parts = [mid[pl.ds(BLOCK * h + row, SUB), :] for h in range(blocks)]
        for h, part in enumerate(butterfly(parts, powers(blocks))):
            emit(BLOCK * h + row, part)
        return carry

    lax.fori_loop(0, BLOCK // SUB, across, 0, unroll=4)


def own_kernel(
    scale, targets, pieces, x_ref, bits_ref, me_ref, source_ref, offset_ref, out_ref, *refs
):
    x, mid, words, sems = refs[-4:]
    rows_dev = x.shape[0]
    me = me_ref[0]
    block = source_ref.shape[1] // targets
    for target in range(0, targets, 2):
        at = pl.multiple_of((me ^ target) * block, math.gcd(128, block))
        source = source_ref[:, pl.ds(at, block)]
        rows = table_row(offset_ref[:, pl.ds(at, block)]) + (source & 1) * rows_dev
        signs = jnp.where(parity(source & me, 16) != 0, -scale, scale)
        for n, (which, start, count) in enumerate(pieces):
            if target in which:
                to = which.index(target) * count
                refs[2 * n][:, to : to + count] = rows[:, start : start + count]
                refs[2 * n + 1][:, to : to + count] = signs[:, start : start + count]

    def emit(row, value):
        out_ref[pl.ds(row, SUB), :] = value

    mix_blocks(x_ref, bits_ref, x, mid, words, sems, emit)


def pair_kernel(x_ref, bits_ref, own_ref, out_ref, x, mid, words, sems):
    count = x.shape[0]

    def emit(row, value):
        own = own_ref[pl.ds(row, SUB), :]
        out_ref[pl.ds(row, SUB), :] = own + value
        out_ref[pl.ds(count + row, SUB), :] = own - value

    mix_blocks(x_ref, bits_ref, x, mid, words, sems, emit)


def pick_kernel(row_ref, sign_ref, table_ref, *refs):
    out_ref = refs[-1]
    count = out_ref.shape[0]
    unroll = math.gcd(count, 32)

    def some(i, carry):
        for u in range(unroll):
            r = i * unroll + u
            out_ref[pl.ds(r, 1), :] = table_ref[pl.ds(row_ref[0, r], 1), :] * sign_ref[0, r]
        return carry

    lax.fori_loop(0, count // unroll, some, 0)


def pick(places, table, after=()):
    rows, signs = places
    count = rows.shape[1]
    vmem = pl.BlockSpec(memory_space=pltpu.VMEM)
    smem = pl.BlockSpec(memory_space=pltpu.SMEM)
    return pl.pallas_call(
        pick_kernel,
        out_shape=jax.ShapeDtypeStruct((count, table.shape[1]), F32),
        in_specs=[smem, smem, vmem] + [pl.BlockSpec(memory_space=pl.ANY)] * len(after),
        out_specs=vmem,
        compiler_params=pltpu.CompilerParams(vmem_limit_bytes=14 * MIB),
        cost_estimate=pl.CostEstimate(
            flops=1024, bytes_accessed=1024, transcendentals=0
        ),
        name="pick",
    )(rows, signs, pltpu.with_memory_space_constraint(table, pltpu.VMEM), *after)


def factor_panel(left, right, next_left, next_right, at):
    shape = left.shape
    rows = lax.broadcasted_iota(I32, shape, 0)

    def lane(x, i):
        return jnp.broadcast_to(x[:, at + i : at + i + 1], shape)

    def row(x, i):
        return jnp.broadcast_to(x[i : i + 1, :], shape)

    more = next_left is not None
    column = [lane(left, i) for i in range(SUB)]
    below = [lane(next_left, i) for i in range(SUB)] if more else []
    pivots = jnp.ones_like(left)
    for i in range(SUB):
        pivot = row(column[i], i)
        pivots = jnp.where(rows == i, pivot, pivots)
        inverse = 1.0 / pivot
        ratio = jnp.where(rows > i, column[i], 0.0) * inverse
        if more:
            next_ratio = below[i] * inverse
        for j in range(i + 1, SUB):
            top = row(column[j], i)
            column[j] = column[j] - ratio * top
            if more:
                below[j] = below[j] - next_ratio * top
        top, unit = row(left, i), row(right, i)
        if more:
            next_left = next_left - next_ratio * top
            next_right = next_right - next_ratio * unit
        if i < SUB - 1:
            left = left - ratio * top
            right = right - ratio * unit
    scale = lax.rsqrt(pivots)
    return left * scale, right * scale, next_left, next_right


def factor(gram):
    n = gram.shape[0]
    unit = (
        lax.broadcasted_iota(I32, (n, n), 0) == lax.broadcasted_iota(I32, (n, n), 1)
    ).astype(F32)
    lanes = lax.broadcasted_iota(I32, (SUB, n), 1)
    panel_rows = lax.broadcasted_iota(I32, (SUB, n), 0)
    left, right = gram[:SUB], unit[:SUB]
    rest, unit = gram[SUB:], unit[SUB:]
    uppers, inverses = [], []
    for at in range(0, n, SUB):
        more = at + SUB < n
        next_left, next_right = (rest[:SUB], unit[:SUB]) if more else (None, None)
        done_left, done_right, left, right = factor_panel(left, right, next_left, next_right, at)
        done_left = jnp.where(lanes >= panel_rows + at, done_left, 0.0)
        uppers.append(done_left)
        inverses.append(done_right)
        rest, unit = rest[SUB:], unit[SUB:]
        if at + 2 * SUB < n:
            h, m, l = split3(done_left)
            uh, um, ul = split3(done_right)
            terms = jnp.concatenate([h, h, m, h, l, m], 0)
            others = jnp.concatenate(
                [
                    jnp.concatenate([h, m, h, l, h, m], 0),
                    jnp.concatenate([uh, um, uh, ul, uh, um], 0),
                ],
                1,
            )
            change = jnp.dot(terms.T[at + 2 * SUB :], others, preferred_element_type=F32)
            rest = rest - change[:, :n]
            unit = unit - change[:, n:]
    return jnp.concatenate(uppers, 0), jnp.concatenate(inverses, 0)


def finish_kernel(gram_ref, sketch_ref, q_ref, upper_ref):
    upper, inverse = factor(gram_ref[...])
    upper_ref[...] = upper
    q_ref[...] = lax.dot_general(
        sketch_ref[...],
        inverse,
        (((1,), (1,)), ((), ())),
        precision=lax.Precision.HIGHEST,
        preferred_element_type=F32,
    )


def per_device(features, sign_bits, sample_device, sample_offset):
    rows_dev, width = features.shape
    n_outer = lax.axis_size("exa")
    n_inner = lax.axis_size("exb")
    n_all = n_outer * n_inner
    bits = n_all.bit_length() - 1
    inner_bits = n_inner.bit_length() - 1
    myself = lax.axis_index("exa") * n_inner + lax.axis_index("exb")
    total = sample_offset.shape[0]
    own_count = total // n_all
    vmem = pl.BlockSpec(memory_space=pltpu.VMEM)

    def swap(value, mask):
        if mask < n_inner:
            return lax.ppermute(value, "exb", bit_perm(n_inner, mask))
        return lax.ppermute(value, "exa", bit_perm(n_outer, mask // n_inner))

    outer = tuple(range(inner_bits, bits))
    inner = [(bit,) for bit in range(1, inner_bits)]
    back = inner[::-1]
    orders = [(16, inner[:1] + [outer[:1]] + inner[1:] + [outer[1:]]), (16, back[:1] + [outer[:1]] + back[1:] + [outer[1:]]), (16, inner + [(bit,) for bit in outer]), (16, back + [(bit,) for bit in outer])]
    chunks, start = [], 0
    for share, steps in orders:
        chunks.append((start, own_count * share // 64, steps))
        start += own_count * share // 64

    def masks(step):
        listed = [0]
        for bit in step:
            listed = [e | 1 << bit for e in listed] + listed
        return listed

    def targets(steps):
        listed = [0]
        for step in steps[::-1]:
            listed = [m | e for m in masks(step) for e in listed]
        return listed

    firsts = []
    for start, count, steps in chunks:
        listed = targets(steps)
        moves = masks(steps[0])
        per = len(listed) // len(moves)
        firsts.append(
            [
                (listed[i * per : i * per + per], start, count)
                for i in range(len(moves))
            ]
        )
    flat = [piece for pieces in firsts for piece in pieces]

    far_features = swap(features, 1)
    far_signs = swap(sign_bits, 1)
    params = pltpu.CompilerParams(vmem_limit_bytes=22 * MIB)
    scratch = [
        pltpu.VMEM((rows_dev, width), F32),
        pltpu.VMEM((rows_dev, width), F32),
        pltpu.VMEM((rows_dev // PER_WORD, width), I32),
        pltpu.SemaphoreType.DMA((rows_dev // BLOCK,)),
    ]
    bits_shape = (rows_dev // 128, 128)
    place_shapes = [
        jax.ShapeDtypeStruct((1, len(which) * count), kind)
        for which, _, count in flat
        for kind in (I32, F32)
    ]
    own, *places = pl.pallas_call(
        functools.partial(own_kernel, 1.0 / math.sqrt(rows_dev * n_all), n_all, flat),
        out_shape=[jax.ShapeDtypeStruct((rows_dev, width), F32)] + place_shapes,
        in_specs=[
            pl.BlockSpec(memory_space=pl.ANY),
            vmem,
            pl.BlockSpec(memory_space=pltpu.SMEM),
            vmem,
            vmem,
        ],
        out_specs=[vmem] * (1 + len(place_shapes)),
        scratch_shapes=scratch,
        compiler_params=params,
        cost_estimate=pl.CostEstimate(flops=10**7, bytes_accessed=12 * MIB, transcendentals=0),
        name="own",
    )(
        pltpu.with_memory_space_constraint(features, pltpu.HBM),
        sign_bits.reshape(bits_shape),
        myself.reshape(1),
        sample_device.reshape(1, total),
        sample_offset.reshape(1, total),
    )
    table = pl.pallas_call(
        pair_kernel,
        out_shape=jax.ShapeDtypeStruct((2 * rows_dev, width), F32),
        in_specs=[pl.BlockSpec(memory_space=pl.ANY), vmem, vmem],
        out_specs=vmem,
        scratch_shapes=scratch,
        compiler_params=params,
        cost_estimate=pl.CostEstimate(flops=10**7, bytes_accessed=16 * MIB, transcendentals=0),
        name="pair",
    )(
        far_features,
        far_signs.reshape(bits_shape),
        pltpu.with_memory_space_constraint(own, pltpu.VMEM),
    )

    pairs = iter(zip(places[::2], places[1::2]))
    mine = [[next(pairs) for _ in pieces] for pieces in firsts]
    sent = [
        [swap(pick(one, table), mask) for one, mask in zip(some[:-1], masks(steps[0]))]
        for some, (_, _, steps) in zip(mine, chunks)
    ]
    waits = [None,None,0,1]
    kept = [
        pick(some[-1], table, () if wait is None else (sent[wait][0],))
        for some, wait in zip(mine, waits)
    ]
    for turn in range(1, max(len(steps) for _, _, steps in chunks) + 1):
        for n, (_, _, steps) in enumerate(chunks):
            if turn > len(steps):
                continue
            sums = functools.reduce(jnp.add, sent[n], kept[n])
            if turn < len(steps):
                listed = masks(steps[turn])
                per = sums.shape[0] // len(listed)
                sent[n] = [
                    swap(sums[i * per : i * per + per], move) for i, move in enumerate(listed[:-1])
                ]
                sums = sums[-per:]
            kept[n] = sums
    sketch = jnp.concatenate(kept, 0)

    gram = lax.dot_general(
        sketch,
        sketch,
        (((0,), (0,)), ((), ())),
        precision=lax.Precision.HIGHEST,
        preferred_element_type=F32,
    ) / total
    groups = [(0,)] + [tuple(range(b, min(b + 2, inner_bits))) for b in range(1, inner_bits, 2)]
    for group in groups + [(bit,) for bit in outer]:
        near = gram + swap(gram, 1 << group[0])
        if len(group) == 2:
            far = 1 << group[1]
            near = near + (swap(gram, far) + swap(gram, far | 1 << group[0]))
        gram = near

    return pl.pallas_call(
        finish_kernel,
        out_shape=(
            jax.ShapeDtypeStruct((own_count, width), F32),
            jax.ShapeDtypeStruct((width, width), F32),
        ),
        in_specs=[vmem, vmem],
        out_specs=(vmem, vmem),
        name="finish",
    )(gram, sketch)


def solution(mesh):
    placed = (P(("exa", "exb"), None), P(("exa", "exb")), P(), P())
    return jax.shard_map(
        per_device,
        mesh=mesh,
        in_specs=placed,
        out_specs=(P(("exa", "exb"), None), P()),
        check_vma=False,
    )
```

```python
import functools
import math

import jax
import jax.numpy as jnp
from jax import lax
from jax.experimental import pallas as pl
from jax.experimental.pallas import tpu as pltpu
from jax.sharding import PartitionSpec as P

F32 = jnp.float32
BF16 = jnp.bfloat16
I32 = jnp.int32
SUB = 8
PER_WORD = 32
GROUP = SUB * PER_WORD
BLOCK = 4 * GROUP
MIB = 1 << 20


def parity(bits, width):
    total = jnp.zeros_like(bits)
    for place in range(width):
        total = total ^ (bits >> place)
    return total & 1


def split3(x):
    high = x.astype(BF16).astype(F32)
    rest = x - high
    mid = rest.astype(BF16).astype(F32)
    return high, mid, rest - mid


def bit_perm(size, bit):
    return [(i, i ^ bit) for i in range(size)]


def butterfly(parts, steps):
    for step in steps:
        mixed = list(parts)
        for i in range(len(parts)):
            if not i & step:
                mixed[i] = parts[i] + parts[i | step]
                mixed[i | step] = parts[i] - parts[i | step]
        parts = mixed
    return parts


def powers(count):
    return [1 << i for i in range(count.bit_length() - 1)]


def word_bit(v):
    return 1 << v if v < 31 else -(1 << 31)


def mix_block(x_ref, word_ref, out_ref, at):
    def signed_group(g, carry):
        base = pl.multiple_of(at + g * GROUP, GROUP)
        words = word_ref[pl.ds(pl.multiple_of(base // PER_WORD, SUB), SUB), :]
        parts = []
        for v in range(PER_WORD):
            part = x_ref[pl.ds(base + SUB * v, SUB), :]
            parts.append(jnp.where((words & word_bit(v)) != 0, part, -part))
        for v, part in enumerate(butterfly(parts, powers(PER_WORD))):
            out_ref[pl.ds(base + SUB * v, SUB), :] = part
        return carry

    lax.fori_loop(0, BLOCK // GROUP, signed_group, 0, unroll=True)

    def within_group(m, carry):
        base = pl.multiple_of(at + m * SUB * SUB, SUB * SUB)
        spots = [GROUP * k for k in range(BLOCK // GROUP)]
        parts = [
            out_ref[pl.ds(base + spot + t, SUB, stride=SUB), :] for spot in spots for t in range(SUB)
        ]
        parts = butterfly(parts, powers(len(parts)))
        for k, spot in enumerate(spots):
            for t in range(SUB):
                out_ref[pl.ds(base + spot + SUB * t, SUB), :] = parts[SUB * k + t]
        return carry

    lax.fori_loop(0, GROUP // (SUB * SUB), within_group, 0, unroll=True)


def spread_signs(bits_ref, word_ref):
    lanes = bits_ref.shape[1]
    at = lax.broadcasted_iota(I32, (SUB, lanes), 1)
    row = lax.broadcasted_iota(I32, (SUB, lanes), 0)
    weights = jnp.where(at % SUB == row, 1 << (at // SUB), 0).astype(F32)
    halves = lax.dot_general(
        weights, bits_ref[...].astype(F32), (((1,), (1,)), ((), ())), preferred_element_type=F32
    ).astype(I32)
    for g in range(word_ref.shape[0] // SUB):
        word = halves[:, 2 * g : 2 * g + 1] | halves[:, 2 * g + 1 : 2 * g + 2] << (lanes // SUB)
        word_ref[SUB * g : SUB * g + SUB, :] = jnp.broadcast_to(word, (SUB, word_ref.shape[1]))


def table_row(row):
    return (row & ~63) | ((row & 7) << 3) | ((row >> 3) & 7)


def mix_blocks(x_ref, bits_ref, x, mid, word_ref, sems, emit):
    blocks = mid.shape[0] // BLOCK

    def fetch(h):
        rows = pl.ds(pl.multiple_of(h * BLOCK, BLOCK), BLOCK)
        return pltpu.make_async_copy(x_ref.at[rows], x.at[rows], sems.at[h])

    for h in range(blocks):
        fetch(h).start()
    spread_signs(bits_ref, word_ref)

    def one(h, carry):
        fetch(h).wait()
        mix_block(x, word_ref, mid, h * BLOCK)
        return carry

    lax.fori_loop(0, blocks, one, 0)

    def across(g, carry):
        row = pl.multiple_of(g * SUB, SUB)
        parts = [mid[pl.ds(BLOCK * h + row, SUB), :] for h in range(blocks)]
        for h, part in enumerate(butterfly(parts, powers(blocks))):
            emit(BLOCK * h + row, part)
        return carry

    lax.fori_loop(0, BLOCK // SUB, across, 0, unroll=4)


def own_kernel(
    scale, targets, pieces, x_ref, bits_ref, me_ref, source_ref, offset_ref, out_ref, *refs
):
    x, mid, words, sems = refs[-4:]
    rows_dev = x.shape[0]
    me = me_ref[0]
    block = source_ref.shape[1] // targets
    for target in range(0, targets, 2):
        at = pl.multiple_of((me ^ target) * block, math.gcd(128, block))
        source = source_ref[:, pl.ds(at, block)]
        rows = table_row(offset_ref[:, pl.ds(at, block)]) + (source & 1) * rows_dev
        signs = jnp.where(parity(source & me, 16) != 0, -scale, scale)
        for n, (which, start, count) in enumerate(pieces):
            if target in which:
                to = which.index(target) * count
                refs[2 * n][:, to : to + count] = rows[:, start : start + count]
                refs[2 * n + 1][:, to : to + count] = signs[:, start : start + count]

    def emit(row, value):
        out_ref[pl.ds(row, SUB), :] = value

    mix_blocks(x_ref, bits_ref, x, mid, words, sems, emit)


def pair_kernel(x_ref, bits_ref, own_ref, out_ref, x, mid, words, sems):
    count = x.shape[0]

    def emit(row, value):
        own = own_ref[pl.ds(row, SUB), :]
        out_ref[pl.ds(row, SUB), :] = own + value
        out_ref[pl.ds(count + row, SUB), :] = own - value

    mix_blocks(x_ref, bits_ref, x, mid, words, sems, emit)


def pick_kernel(row_ref, sign_ref, table_ref, *refs):
    out_ref = refs[-1]
    count = out_ref.shape[0]
    unroll = math.gcd(count, 32)

    def some(i, carry):
        for u in range(unroll):
            r = i * unroll + u
            out_ref[pl.ds(r, 1), :] = table_ref[pl.ds(row_ref[0, r], 1), :] * sign_ref[0, r]
        return carry

    lax.fori_loop(0, count // unroll, some, 0)


def pick(places, table, after=()):
    rows, signs = places
    count = rows.shape[1]
    vmem = pl.BlockSpec(memory_space=pltpu.VMEM)
    smem = pl.BlockSpec(memory_space=pltpu.SMEM)
    return pl.pallas_call(
        pick_kernel,
        out_shape=jax.ShapeDtypeStruct((count, table.shape[1]), F32),
        in_specs=[smem, smem, vmem] + [pl.BlockSpec(memory_space=pl.ANY)] * len(after),
        out_specs=vmem,
        compiler_params=pltpu.CompilerParams(vmem_limit_bytes=14 * MIB),
        cost_estimate=pl.CostEstimate(
            flops=1024, bytes_accessed=1024, transcendentals=0
        ),
        name="pick",
    )(rows, signs, pltpu.with_memory_space_constraint(table, pltpu.VMEM), *after)


def factor_panel(left, right, next_left, next_right, at):
    shape = left.shape
    rows = lax.broadcasted_iota(I32, shape, 0)

    def lane(x, i):
        return jnp.broadcast_to(x[:, at + i : at + i + 1], shape)

    def row(x, i):
        return jnp.broadcast_to(x[i : i + 1, :], shape)

    more = next_left is not None
    column = [lane(left, i) for i in range(SUB)]
    below = [lane(next_left, i) for i in range(SUB)] if more else []
    pivots = jnp.ones_like(left)
    for i in range(SUB):
        pivot = row(column[i], i)
        pivots = jnp.where(rows == i, pivot, pivots)
        inverse = 1.0 / pivot
        ratio = jnp.where(rows > i, column[i], 0.0) * inverse
        if more:
            next_ratio = below[i] * inverse
        for j in range(i + 1, SUB):
            top = row(column[j], i)
            column[j] = column[j] - ratio * top
            if more:
                below[j] = below[j] - next_ratio * top
        top, unit = row(left, i), row(right, i)
        if more:
            next_left = next_left - next_ratio * top
            next_right = next_right - next_ratio * unit
        if i < SUB - 1:
            left = left - ratio * top
            right = right - ratio * unit
    scale = lax.rsqrt(pivots)
    return left * scale, right * scale, next_left, next_right


def factor(gram):
    n = gram.shape[0]
    unit = (
        lax.broadcasted_iota(I32, (n, n), 0) == lax.broadcasted_iota(I32, (n, n), 1)
    ).astype(F32)
    lanes = lax.broadcasted_iota(I32, (SUB, n), 1)
    panel_rows = lax.broadcasted_iota(I32, (SUB, n), 0)
    left, right = gram[:SUB], unit[:SUB]
    rest, unit = gram[SUB:], unit[SUB:]
    uppers, inverses = [], []
    for at in range(0, n, SUB):
        more = at + SUB < n
        next_left, next_right = (rest[:SUB], unit[:SUB]) if more else (None, None)
        done_left, done_right, left, right = factor_panel(left, right, next_left, next_right, at)
        done_left = jnp.where(lanes >= panel_rows + at, done_left, 0.0)
        uppers.append(done_left)
        inverses.append(done_right)
        rest, unit = rest[SUB:], unit[SUB:]
        if at + 2 * SUB < n:
            h, m, l = split3(done_left)
            uh, um, ul = split3(done_right)
            terms = jnp.concatenate([h, h, m, h, l, m], 0)
            others = jnp.concatenate(
                [
                    jnp.concatenate([h, m, h, l, h, m], 0),
                    jnp.concatenate([uh, um, uh, ul, uh, um], 0),
                ],
                1,
            )
            change = jnp.dot(terms.T[at + 2 * SUB :], others, preferred_element_type=F32)
            rest = rest - change[:, :n]
            unit = unit - change[:, n:]
    return jnp.concatenate(uppers, 0), jnp.concatenate(inverses, 0)


def finish_kernel(gram_ref, far_ref, sketch_ref, q_ref, upper_ref):
    upper, inverse = factor(gram_ref[...] + far_ref[...])
    upper_ref[...] = upper
    q_ref[...] = lax.dot_general(
        sketch_ref[...],
        inverse,
        (((1,), (1,)), ((), ())),
        precision=lax.Precision.HIGHEST,
        preferred_element_type=F32,
    )


def per_device(features, sign_bits, sample_device, sample_offset):
    rows_dev, width = features.shape
    n_outer = lax.axis_size("exa")
    n_inner = lax.axis_size("exb")
    n_all = n_outer * n_inner
    bits = n_all.bit_length() - 1
    inner_bits = n_inner.bit_length() - 1
    myself = lax.axis_index("exa") * n_inner + lax.axis_index("exb")
    total = sample_offset.shape[0]
    own_count = total // n_all
    vmem = pl.BlockSpec(memory_space=pltpu.VMEM)

    def swap(value, mask):
        if mask < n_inner:
            return lax.ppermute(value, "exb", bit_perm(n_inner, mask))
        return lax.ppermute(value, "exa", bit_perm(n_outer, mask // n_inner))

    outer = tuple(range(inner_bits, bits))
    inner = [(bit,) for bit in range(1, inner_bits)]
    back = inner[::-1]
    orders = [(16, inner[:1] + [outer[:1]] + inner[1:] + [outer[1:]]), (16, back[:1] + [outer[:1]] + back[1:] + [outer[1:]]), (16, inner + [(bit,) for bit in outer]), (16, back + [(bit,) for bit in outer])]
    chunks, start = [], 0
    for share, steps in orders:
        chunks.append((start, own_count * share // 64, steps))
        start += own_count * share // 64

    def masks(step):
        listed = [0]
        for bit in step:
            listed = [e | 1 << bit for e in listed] + listed
        return listed

    def targets(steps):
        listed = [0]
        for step in steps[::-1]:
            listed = [m | e for m in masks(step) for e in listed]
        return listed

    firsts = []
    for start, count, steps in chunks:
        listed = targets(steps)
        moves = masks(steps[0])
        per = len(listed) // len(moves)
        firsts.append(
            [
                (listed[i * per : i * per + per], start, count)
                for i in range(len(moves))
            ]
        )
    flat = [piece for pieces in firsts for piece in pieces]

    far_features = swap(features, 1)
    far_signs = swap(sign_bits, 1)
    params = pltpu.CompilerParams(vmem_limit_bytes=22 * MIB)
    scratch = [
        pltpu.VMEM((rows_dev, width), F32),
        pltpu.VMEM((rows_dev, width), F32),
        pltpu.VMEM((rows_dev // PER_WORD, width), I32),
        pltpu.SemaphoreType.DMA((rows_dev // BLOCK,)),
    ]
    bits_shape = (rows_dev // 128, 128)
    place_shapes = [
        jax.ShapeDtypeStruct((1, len(which) * count), kind)
        for which, _, count in flat
        for kind in (I32, F32)
    ]
    own, *places = pl.pallas_call(
        functools.partial(own_kernel, 1.0 / math.sqrt(rows_dev * n_all), n_all, flat),
        out_shape=[jax.ShapeDtypeStruct((rows_dev, width), F32)] + place_shapes,
        in_specs=[
            pl.BlockSpec(memory_space=pl.ANY),
            vmem,
            pl.BlockSpec(memory_space=pltpu.SMEM),
            vmem,
            vmem,
        ],
        out_specs=[vmem] * (1 + len(place_shapes)),
        scratch_shapes=scratch,
        compiler_params=params,
        cost_estimate=pl.CostEstimate(flops=10**7, bytes_accessed=12 * MIB, transcendentals=0),
        name="own",
    )(
        pltpu.with_memory_space_constraint(features, pltpu.HBM),
        sign_bits.reshape(bits_shape),
        myself.reshape(1),
        sample_device.reshape(1, total),
        sample_offset.reshape(1, total),
    )
    table = pl.pallas_call(
        pair_kernel,
        out_shape=jax.ShapeDtypeStruct((2 * rows_dev, width), F32),
        in_specs=[pl.BlockSpec(memory_space=pl.ANY), vmem, vmem],
        out_specs=vmem,
        scratch_shapes=scratch,
        compiler_params=params,
        cost_estimate=pl.CostEstimate(flops=10**7, bytes_accessed=16 * MIB, transcendentals=0),
        name="pair",
    )(
        far_features,
        far_signs.reshape(bits_shape),
        pltpu.with_memory_space_constraint(own, pltpu.VMEM),
    )

    pairs = iter(zip(places[::2], places[1::2]))
    mine = [[next(pairs) for _ in pieces] for pieces in firsts]
    sent = [
        [swap(pick(one, table), mask) for one, mask in zip(some[:-1], masks(steps[0]))]
        for some, (_, _, steps) in zip(mine, chunks)
    ]
    waits = [None,None,0,1]
    kept = [
        pick(some[-1], table, () if wait is None else (sent[wait][0],))
        for some, wait in zip(mine, waits)
    ]
    for turn in range(1, max(len(steps) for _, _, steps in chunks) + 1):
        for n, (_, _, steps) in enumerate(chunks):
            if turn > len(steps):
                continue
            sums = functools.reduce(jnp.add, sent[n], kept[n])
            if turn < len(steps):
                listed = masks(steps[turn])
                per = sums.shape[0] // len(listed)
                sent[n] = [
                    swap(sums[i * per : i * per + per], move) for i, move in enumerate(listed[:-1])
                ]
                sums = sums[-per:]
            kept[n] = sums
    sketch = jnp.concatenate(kept, 0)

    gram = lax.dot_general(
        sketch,
        sketch,
        (((0,), (0,)), ((), ())),
        precision=lax.Precision.HIGHEST,
        preferred_element_type=F32,
    ) / total
    groups = [(0,)] + [tuple(range(b, min(b + 2, inner_bits))) for b in range(1, inner_bits, 2)]
    for group in groups + [(bit,) for bit in outer[:-1]]:
        near = gram + swap(gram, 1 << group[0])
        if len(group) == 2:
            far = 1 << group[1]
            near = near + (swap(gram, far) + swap(gram, far | 1 << group[0]))
        gram = near

    return pl.pallas_call(
        finish_kernel,
        out_shape=(
            jax.ShapeDtypeStruct((own_count, width), F32),
            jax.ShapeDtypeStruct((width, width), F32),
        ),
        in_specs=[vmem, vmem, vmem],
        out_specs=(vmem, vmem),
        name="finish",
    )(gram, pltpu.with_memory_space_constraint(swap(gram, 1 << outer[-1]), pltpu.VMEM), sketch)


def solution(mesh):
    placed = (P(("exa", "exb"), None), P(("exa", "exb")), P(), P())
    return jax.shard_map(
        per_device,
        mesh=mesh,
        in_specs=placed,
        out_specs=(P(("exa", "exb"), None), P()),
        check_vma=False,
    )
```

```python
import functools
import math

import jax
import jax.numpy as jnp
from jax import lax
from jax.experimental import pallas as pl
from jax.experimental.pallas import tpu as pltpu
from jax.sharding import PartitionSpec as P

F32 = jnp.float32
BF16 = jnp.bfloat16
I32 = jnp.int32
SUB = 8
PER_WORD = 32
GROUP = SUB * PER_WORD
BLOCK = 4 * GROUP
MIB = 1 << 20


def parity(bits, width):
    total = jnp.zeros_like(bits)
    for place in range(width):
        total = total ^ (bits >> place)
    return total & 1


def split3(x):
    high = x.astype(BF16).astype(F32)
    rest = x - high
    mid = rest.astype(BF16).astype(F32)
    return high, mid, rest - mid


def bit_perm(size, bit):
    return [(i, i ^ bit) for i in range(size)]


def butterfly(parts, steps):
    for step in steps:
        mixed = list(parts)
        for i in range(len(parts)):
            if not i & step:
                mixed[i] = parts[i] + parts[i | step]
                mixed[i | step] = parts[i] - parts[i | step]
        parts = mixed
    return parts


def powers(count):
    return [1 << i for i in range(count.bit_length() - 1)]


def word_bit(v):
    return 1 << v if v < 31 else -(1 << 31)


def mix_block(x_ref, word_ref, out_ref, at):
    def signed_group(g, carry):
        base = pl.multiple_of(at + g * GROUP, GROUP)
        words = word_ref[pl.ds(pl.multiple_of(base // PER_WORD, SUB), SUB), :]
        parts = []
        for v in range(PER_WORD):
            part = x_ref[pl.ds(base + SUB * v, SUB), :]
            parts.append(jnp.where((words & word_bit(v)) != 0, part, -part))
        for v, part in enumerate(butterfly(parts, powers(PER_WORD))):
            out_ref[pl.ds(base + SUB * v, SUB), :] = part
        return carry

    lax.fori_loop(0, BLOCK // GROUP, signed_group, 0, unroll=True)

    def within_group(m, carry):
        base = pl.multiple_of(at + m * SUB * SUB, SUB * SUB)
        spots = [GROUP * k for k in range(BLOCK // GROUP)]
        parts = [
            out_ref[pl.ds(base + spot + t, SUB, stride=SUB), :] for spot in spots for t in range(SUB)
        ]
        parts = butterfly(parts, powers(len(parts)))
        for k, spot in enumerate(spots):
            for t in range(SUB):
                out_ref[pl.ds(base + spot + SUB * t, SUB), :] = parts[SUB * k + t]
        return carry

    lax.fori_loop(0, GROUP // (SUB * SUB), within_group, 0, unroll=True)


def spread_signs(bits_ref, word_ref):
    lanes = bits_ref.shape[1]
    at = lax.broadcasted_iota(I32, (SUB, lanes), 1)
    row = lax.broadcasted_iota(I32, (SUB, lanes), 0)
    weights = jnp.where(at % SUB == row, 1 << (at // SUB), 0).astype(F32)
    halves = lax.dot_general(
        weights, bits_ref[...].astype(F32), (((1,), (1,)), ((), ())), preferred_element_type=F32
    ).astype(I32)
    for g in range(word_ref.shape[0] // SUB):
        word = halves[:, 2 * g : 2 * g + 1] | halves[:, 2 * g + 1 : 2 * g + 2] << (lanes // SUB)
        word_ref[SUB * g : SUB * g + SUB, :] = jnp.broadcast_to(word, (SUB, word_ref.shape[1]))


def table_row(row):
    return (row & ~63) | ((row & 7) << 3) | ((row >> 3) & 7)


def mix_blocks(x_ref, bits_ref, x, mid, word_ref, sems, emit):
    blocks = mid.shape[0] // BLOCK

    def fetch(h):
        rows = pl.ds(pl.multiple_of(h * BLOCK, BLOCK), BLOCK)
        return pltpu.make_async_copy(x_ref.at[rows], x.at[rows], sems.at[h])

    for h in range(blocks):
        fetch(h).start()
    spread_signs(bits_ref, word_ref)

    def one(h, carry):
        fetch(h).wait()
        mix_block(x, word_ref, mid, h * BLOCK)
        return carry

    lax.fori_loop(0, blocks, one, 0)

    def across(g, carry):
        row = pl.multiple_of(g * SUB, SUB)
        parts = [mid[pl.ds(BLOCK * h + row, SUB), :] for h in range(blocks)]
        for h, part in enumerate(butterfly(parts, powers(blocks))):
            emit(BLOCK * h + row, part)
        return carry

    lax.fori_loop(0, BLOCK // SUB, across, 0, unroll=4)


def own_kernel(
    scale, targets, pieces, x_ref, bits_ref, me_ref, source_ref, offset_ref, out_ref, *refs
):
    x, mid, words, sems = refs[-4:]
    rows_dev = x.shape[0]
    me = me_ref[0]
    block = source_ref.shape[1] // targets
    for target in range(0, targets, 2):
        at = pl.multiple_of((me ^ target) * block, math.gcd(128, block))
        source = source_ref[:, pl.ds(at, block)]
        rows = table_row(offset_ref[:, pl.ds(at, block)]) + (source & 1) * rows_dev
        signs = jnp.where(parity(source & me, 16) != 0, -scale, scale)
        for n, (which, start, count) in enumerate(pieces):
            if target in which:
                to = which.index(target) * count
                refs[2 * n][:, to : to + count] = rows[:, start : start + count]
                refs[2 * n + 1][:, to : to + count] = signs[:, start : start + count]

    def emit(row, value):
        out_ref[pl.ds(row, SUB), :] = value

    mix_blocks(x_ref, bits_ref, x, mid, words, sems, emit)


def pair_kernel(x_ref, bits_ref, own_ref, out_ref, x, mid, words, sems):
    count = x.shape[0]

    def emit(row, value):
        own = own_ref[pl.ds(row, SUB), :]
        out_ref[pl.ds(row, SUB), :] = own + value
        out_ref[pl.ds(count + row, SUB), :] = own - value

    mix_blocks(x_ref, bits_ref, x, mid, words, sems, emit)


def pick_kernel(row_ref, sign_ref, table_ref, *refs):
    out_ref = refs[-1]
    count = out_ref.shape[0]
    unroll = math.gcd(count, 64)

    def some(i, carry):
        for u in range(unroll):
            r = i * unroll + u
            out_ref[pl.ds(r, 1), :] = table_ref[pl.ds(row_ref[0, r], 1), :] * sign_ref[0, r]
        return carry

    lax.fori_loop(0, count // unroll, some, 0)


def pick(places, table, after=()):
    rows, signs = places
    count = rows.shape[1]
    vmem = pl.BlockSpec(memory_space=pltpu.VMEM)
    smem = pl.BlockSpec(memory_space=pltpu.SMEM)
    return pl.pallas_call(
        pick_kernel,
        out_shape=jax.ShapeDtypeStruct((count, table.shape[1]), F32),
        in_specs=[smem, smem, vmem] + [pl.BlockSpec(memory_space=pl.ANY)] * len(after),
        out_specs=vmem,
        compiler_params=pltpu.CompilerParams(vmem_limit_bytes=14 * MIB),
        cost_estimate=pl.CostEstimate(
            flops=1024, bytes_accessed=1024, transcendentals=0
        ),
        name="pick",
    )(rows, signs, pltpu.with_memory_space_constraint(table, pltpu.VMEM), *after)


def factor_panel(left, right, next_left, next_right, at):
    shape = left.shape
    rows = lax.broadcasted_iota(I32, shape, 0)

    def lane(x, i):
        return jnp.broadcast_to(x[:, at + i : at + i + 1], shape)

    def row(x, i):
        return jnp.broadcast_to(x[i : i + 1, :], shape)

    more = next_left is not None
    column = [lane(left, i) for i in range(SUB)]
    below = [lane(next_left, i) for i in range(SUB)] if more else []
    pivots = jnp.ones_like(left)
    for i in range(SUB):
        pivot = row(column[i], i)
        pivots = jnp.where(rows == i, pivot, pivots)
        inverse = 1.0 / pivot
        ratio = jnp.where(rows > i, column[i], 0.0) * inverse
        if more:
            next_ratio = below[i] * inverse
        for j in range(i + 1, SUB):
            top = row(column[j], i)
            column[j] = column[j] - ratio * top
            if more:
                below[j] = below[j] - next_ratio * top
        top, unit = row(left, i), row(right, i)
        if more:
            next_left = next_left - next_ratio * top
            next_right = next_right - next_ratio * unit
        if i < SUB - 1:
            left = left - ratio * top
            right = right - ratio * unit
    scale = lax.rsqrt(pivots)
    return left * scale, right * scale, next_left, next_right


def factor(gram):
    n = gram.shape[0]
    unit = (
        lax.broadcasted_iota(I32, (n, n), 0) == lax.broadcasted_iota(I32, (n, n), 1)
    ).astype(F32)
    lanes = lax.broadcasted_iota(I32, (SUB, n), 1)
    panel_rows = lax.broadcasted_iota(I32, (SUB, n), 0)
    left, right = gram[:SUB], unit[:SUB]
    rest, unit = gram[SUB:], unit[SUB:]
    uppers, inverses = [], []
    for at in range(0, n, SUB):
        more = at + SUB < n
        next_left, next_right = (rest[:SUB], unit[:SUB]) if more else (None, None)
        done_left, done_right, left, right = factor_panel(left, right, next_left, next_right, at)
        done_left = jnp.where(lanes >= panel_rows + at, done_left, 0.0)
        uppers.append(done_left)
        inverses.append(done_right)
        rest, unit = rest[SUB:], unit[SUB:]
        if at + 2 * SUB < n:
            h, m, l = split3(done_left)
            uh, um, ul = split3(done_right)
            terms = jnp.concatenate([h, h, m, h, l, m], 0)
            others = jnp.concatenate(
                [
                    jnp.concatenate([h, m, h, l, h, m], 0),
                    jnp.concatenate([uh, um, uh, ul, uh, um], 0),
                ],
                1,
            )
            change = jnp.dot(terms.T[at + 2 * SUB :], others, preferred_element_type=F32)
            rest = rest - change[:, :n]
            unit = unit - change[:, n:]
    return jnp.concatenate(uppers, 0), jnp.concatenate(inverses, 0)


def finish_kernel(gram_ref, far_ref, sketch_ref, q_ref, upper_ref):
    upper, inverse = factor(gram_ref[...] + far_ref[...])
    upper_ref[...] = upper
    q_ref[...] = lax.dot_general(
        sketch_ref[...],
        inverse,
        (((1,), (1,)), ((), ())),
        precision=lax.Precision.HIGHEST,
        preferred_element_type=F32,
    )


def per_device(features, sign_bits, sample_device, sample_offset):
    rows_dev, width = features.shape
    n_outer = lax.axis_size("exa")
    n_inner = lax.axis_size("exb")
    n_all = n_outer * n_inner
    bits = n_all.bit_length() - 1
    inner_bits = n_inner.bit_length() - 1
    myself = lax.axis_index("exa") * n_inner + lax.axis_index("exb")
    total = sample_offset.shape[0]
    own_count = total // n_all
    vmem = pl.BlockSpec(memory_space=pltpu.VMEM)

    def swap(value, mask):
        if mask < n_inner:
            return lax.ppermute(value, "exb", bit_perm(n_inner, mask))
        return lax.ppermute(value, "exa", bit_perm(n_outer, mask // n_inner))

    outer = tuple(range(inner_bits, bits))
    inner = [(bit,) for bit in range(1, inner_bits)]
    back = inner[::-1]
    orders = [(16, inner[:1] + [outer[:1]] + inner[1:] + [outer[1:]]), (16, back[:1] + [outer[:1]] + back[1:] + [outer[1:]]), (16, inner + [(bit,) for bit in outer]), (16, back + [(bit,) for bit in outer])]
    chunks, start = [], 0
    for share, steps in orders:
        chunks.append((start, own_count * share // 64, steps))
        start += own_count * share // 64

    def masks(step):
        listed = [0]
        for bit in step:
            listed = [e | 1 << bit for e in listed] + listed
        return listed

    def targets(steps):
        listed = [0]
        for step in steps[::-1]:
            listed = [m | e for m in masks(step) for e in listed]
        return listed

    firsts = []
    for start, count, steps in chunks:
        listed = targets(steps)
        moves = masks(steps[0])
        per = len(listed) // len(moves)
        firsts.append(
            [
                (listed[i * per : i * per + per], start, count)
                for i in range(len(moves))
            ]
        )
    flat = [piece for pieces in firsts for piece in pieces]

    far_features = swap(features, 1)
    far_signs = swap(sign_bits, 1)
    params = pltpu.CompilerParams(vmem_limit_bytes=22 * MIB)
    scratch = [
        pltpu.VMEM((rows_dev, width), F32),
        pltpu.VMEM((rows_dev, width), F32),
        pltpu.VMEM((rows_dev // PER_WORD, width), I32),
        pltpu.SemaphoreType.DMA((rows_dev // BLOCK,)),
    ]
    bits_shape = (rows_dev // 128, 128)
    place_shapes = [
        jax.ShapeDtypeStruct((1, len(which) * count), kind)
        for which, _, count in flat
        for kind in (I32, F32)
    ]
    own, *places = pl.pallas_call(
        functools.partial(own_kernel, 1.0 / math.sqrt(rows_dev * n_all), n_all, flat),
        out_shape=[jax.ShapeDtypeStruct((rows_dev, width), F32)] + place_shapes,
        in_specs=[
            pl.BlockSpec(memory_space=pl.ANY),
            vmem,
            pl.BlockSpec(memory_space=pltpu.SMEM),
            vmem,
            vmem,
        ],
        out_specs=[vmem] * (1 + len(place_shapes)),
        scratch_shapes=scratch,
        compiler_params=params,
        cost_estimate=pl.CostEstimate(flops=10**7, bytes_accessed=12 * MIB, transcendentals=0),
        name="own",
    )(
        pltpu.with_memory_space_constraint(features, pltpu.HBM),
        sign_bits.reshape(bits_shape),
        myself.reshape(1),
        sample_device.reshape(1, total),
        sample_offset.reshape(1, total),
    )
    table = pl.pallas_call(
        pair_kernel,
        out_shape=jax.ShapeDtypeStruct((2 * rows_dev, width), F32),
        in_specs=[pl.BlockSpec(memory_space=pl.ANY), vmem, vmem],
        out_specs=vmem,
        scratch_shapes=scratch,
        compiler_params=params,
        cost_estimate=pl.CostEstimate(flops=10**7, bytes_accessed=16 * MIB, transcendentals=0),
        name="pair",
    )(
        far_features,
        far_signs.reshape(bits_shape),
        pltpu.with_memory_space_constraint(own, pltpu.VMEM),
    )

    pairs = iter(zip(places[::2], places[1::2]))
    mine = [[next(pairs) for _ in pieces] for pieces in firsts]
    sent = [
        [swap(pick(one, table), mask) for one, mask in zip(some[:-1], masks(steps[0]))]
        for some, (_, _, steps) in zip(mine, chunks)
    ]
    waits = [None,None,0,1]
    kept = [
        pick(some[-1], table, () if wait is None else (sent[wait][0],))
        for some, wait in zip(mine, waits)
    ]
    for turn in range(1, max(len(steps) for _, _, steps in chunks) + 1):
        for n, (_, _, steps) in enumerate(chunks):
            if turn > len(steps):
                continue
            sums = functools.reduce(jnp.add, sent[n], kept[n])
            if turn < len(steps):
                listed = masks(steps[turn])
                per = sums.shape[0] // len(listed)
                sent[n] = [
                    swap(sums[i * per : i * per + per], move) for i, move in enumerate(listed[:-1])
                ]
                sums = sums[-per:]
            kept[n] = sums
    sketch = jnp.concatenate(kept, 0)

    gram = lax.dot_general(
        sketch,
        sketch,
        (((0,), (0,)), ((), ())),
        precision=lax.Precision.HIGHEST,
        preferred_element_type=F32,
    ) / total
    groups = [(0,)] + [tuple(range(b, min(b + 2, inner_bits))) for b in range(1, inner_bits, 2)]
    for group in groups + [(bit,) for bit in outer[1:]]:
        near = gram + swap(gram, 1 << group[0])
        if len(group) == 2:
            far = 1 << group[1]
            near = near + (swap(gram, far) + swap(gram, far | 1 << group[0]))
        gram = near

    return pl.pallas_call(
        finish_kernel,
        out_shape=(
            jax.ShapeDtypeStruct((own_count, width), F32),
            jax.ShapeDtypeStruct((width, width), F32),
        ),
        in_specs=[vmem, vmem, vmem],
        out_specs=(vmem, vmem),
        name="finish",
    )(gram, pltpu.with_memory_space_constraint(swap(gram, 1 << outer[0]), pltpu.VMEM), sketch)


def solution(mesh):
    placed = (P(("exa", "exb"), None), P(("exa", "exb")), P(), P())
    return jax.shard_map(
        per_device,
        mesh=mesh,
        in_specs=placed,
        out_specs=(P(("exa", "exb"), None), P()),
        check_vma=False,
    )
```

```python
import functools
import math

import jax
import jax.numpy as jnp
from jax import lax
from jax.experimental import pallas as pl
from jax.experimental.pallas import tpu as pltpu
from jax.sharding import PartitionSpec as P

F32 = jnp.float32
BF16 = jnp.bfloat16
I32 = jnp.int32
SUB = 8
PER_WORD = 32
GROUP = SUB * PER_WORD
BLOCK = 4 * GROUP
MIB = 1 << 20


def parity(bits, width):
    total = jnp.zeros_like(bits)
    for place in range(width):
        total = total ^ (bits >> place)
    return total & 1


def split3(x):
    high = x.astype(BF16).astype(F32)
    rest = x - high
    mid = rest.astype(BF16).astype(F32)
    return high, mid, rest - mid


def bit_perm(size, bit):
    return [(i, i ^ bit) for i in range(size)]


def butterfly(parts, steps):
    for step in steps:
        mixed = list(parts)
        for i in range(len(parts)):
            if not i & step:
                mixed[i] = parts[i] + parts[i | step]
                mixed[i | step] = parts[i] - parts[i | step]
        parts = mixed
    return parts


def powers(count):
    return [1 << i for i in range(count.bit_length() - 1)]


def word_bit(v):
    return 1 << v if v < 31 else -(1 << 31)


def mix_block(x_ref, word_ref, out_ref, at):
    def signed_group(g, carry):
        base = pl.multiple_of(at + g * GROUP, GROUP)
        words = word_ref[pl.ds(pl.multiple_of(base // PER_WORD, SUB), SUB), :]
        parts = []
        for v in range(PER_WORD):
            part = x_ref[pl.ds(base + SUB * v, SUB), :]
            parts.append(jnp.where((words & word_bit(v)) != 0, part, -part))
        for v, part in enumerate(butterfly(parts, powers(PER_WORD))):
            out_ref[pl.ds(base + SUB * v, SUB), :] = part
        return carry

    lax.fori_loop(0, BLOCK // GROUP, signed_group, 0, unroll=True)

    def within_group(m, carry):
        base = pl.multiple_of(at + m * SUB * SUB, SUB * SUB)
        spots = [GROUP * k for k in range(BLOCK // GROUP)]
        parts = [
            out_ref[pl.ds(base + spot + t, SUB, stride=SUB), :] for spot in spots for t in range(SUB)
        ]
        parts = butterfly(parts, powers(len(parts)))
        for k, spot in enumerate(spots):
            for t in range(SUB):
                out_ref[pl.ds(base + spot + SUB * t, SUB), :] = parts[SUB * k + t]
        return carry

    lax.fori_loop(0, GROUP // (SUB * SUB), within_group, 0, unroll=True)


def spread_signs(bits_ref, word_ref):
    lanes = bits_ref.shape[1]
    at = lax.broadcasted_iota(I32, (SUB, lanes), 1)
    row = lax.broadcasted_iota(I32, (SUB, lanes), 0)
    weights = jnp.where(at % SUB == row, 1 << (at // SUB), 0).astype(F32)
    halves = lax.dot_general(
        weights, bits_ref[...].astype(F32), (((1,), (1,)), ((), ())), preferred_element_type=F32
    ).astype(I32)
    for g in range(word_ref.shape[0] // SUB):
        word = halves[:, 2 * g : 2 * g + 1] | halves[:, 2 * g + 1 : 2 * g + 2] << (lanes // SUB)
        word_ref[SUB * g : SUB * g + SUB, :] = jnp.broadcast_to(word, (SUB, word_ref.shape[1]))


def table_row(row):
    return (row & ~63) | ((row & 7) << 3) | ((row >> 3) & 7)


def mix_blocks(x_ref, bits_ref, x, mid, word_ref, sems, emit):
    blocks = mid.shape[0] // BLOCK

    def fetch(h):
        rows = pl.ds(pl.multiple_of(h * BLOCK, BLOCK), BLOCK)
        return pltpu.make_async_copy(x_ref.at[rows], x.at[rows], sems.at[h])

    for h in range(blocks):
        fetch(h).start()
    spread_signs(bits_ref, word_ref)

    def one(h, carry):
        fetch(h).wait()
        mix_block(x, word_ref, mid, h * BLOCK)
        return carry

    lax.fori_loop(0, blocks, one, 0)

    def across(g, carry):
        row = pl.multiple_of(g * SUB, SUB)
        parts = [mid[pl.ds(BLOCK * h + row, SUB), :] for h in range(blocks)]
        for h, part in enumerate(butterfly(parts, powers(blocks))):
            emit(BLOCK * h + row, part)
        return carry

    lax.fori_loop(0, BLOCK // SUB, across, 0, unroll=8)


def own_kernel(
    scale, targets, pieces, x_ref, bits_ref, me_ref, source_ref, offset_ref, out_ref, *refs
):
    x, mid, words, sems = refs[-4:]
    rows_dev = x.shape[0]
    me = me_ref[0]
    block = source_ref.shape[1] // targets
    for target in range(0, targets, 2):
        at = pl.multiple_of((me ^ target) * block, math.gcd(128, block))
        source = source_ref[:, pl.ds(at, block)]
        rows = table_row(offset_ref[:, pl.ds(at, block)]) + (source & 1) * rows_dev
        signs = jnp.where(parity(source & me, 16) != 0, -scale, scale)
        for n, (which, start, count) in enumerate(pieces):
            if target in which:
                to = which.index(target) * count
                refs[2 * n][:, to : to + count] = rows[:, start : start + count]
                refs[2 * n + 1][:, to : to + count] = signs[:, start : start + count]

    def emit(row, value):
        out_ref[pl.ds(row, SUB), :] = value

    mix_blocks(x_ref, bits_ref, x, mid, words, sems, emit)


def pair_kernel(x_ref, bits_ref, own_ref, out_ref, x, mid, words, sems):
    count = x.shape[0]

    def emit(row, value):
        own = own_ref[pl.ds(row, SUB), :]
        out_ref[pl.ds(row, SUB), :] = own + value
        out_ref[pl.ds(count + row, SUB), :] = own - value

    mix_blocks(x_ref, bits_ref, x, mid, words, sems, emit)


def pick_kernel(row_ref, sign_ref, table_ref, *refs):
    out_ref = refs[-1]
    count = out_ref.shape[0]
    unroll = math.gcd(count, 128)

    def some(i, carry):
        for u in range(unroll):
            r = i * unroll + u
            out_ref[pl.ds(r, 1), :] = table_ref[pl.ds(row_ref[0, r], 1), :] * sign_ref[0, r]
        return carry

    lax.fori_loop(0, count // unroll, some, 0)


def pick(places, table, after=()):
    rows, signs = places
    count = rows.shape[1]
    vmem = pl.BlockSpec(memory_space=pltpu.VMEM)
    smem = pl.BlockSpec(memory_space=pltpu.SMEM)
    return pl.pallas_call(
        pick_kernel,
        out_shape=jax.ShapeDtypeStruct((count, table.shape[1]), F32),
        in_specs=[smem, smem, vmem] + [pl.BlockSpec(memory_space=pl.ANY)] * len(after),
        out_specs=vmem,
        compiler_params=pltpu.CompilerParams(vmem_limit_bytes=14 * MIB),
        cost_estimate=pl.CostEstimate(
            flops=1024, bytes_accessed=1024, transcendentals=0
        ),
        name="pick",
    )(rows, signs, pltpu.with_memory_space_constraint(table, pltpu.VMEM), *after)


def factor_panel(left, right, next_left, next_right, at):
    shape = left.shape
    rows = lax.broadcasted_iota(I32, shape, 0)

    def lane(x, i):
        return jnp.broadcast_to(x[:, at + i : at + i + 1], shape)

    def row(x, i):
        return jnp.broadcast_to(x[i : i + 1, :], shape)

    more = next_left is not None
    column = [lane(left, i) for i in range(SUB)]
    below = [lane(next_left, i) for i in range(SUB)] if more else []
    pivots = jnp.ones_like(left)
    for i in range(SUB):
        pivot = row(column[i], i)
        pivots = jnp.where(rows == i, pivot, pivots)
        inverse = 1.0 / pivot
        ratio = jnp.where(rows > i, column[i], 0.0) * inverse
        if more:
            next_ratio = below[i] * inverse
        for j in range(i + 1, SUB):
            top = row(column[j], i)
            column[j] = column[j] - ratio * top
            if more:
                below[j] = below[j] - next_ratio * top
        top, unit = row(left, i), row(right, i)
        if more:
            next_left = next_left - next_ratio * top
            next_right = next_right - next_ratio * unit
        if i < SUB - 1:
            left = left - ratio * top
            right = right - ratio * unit
    scale = lax.rsqrt(pivots)
    return left * scale, right * scale, next_left, next_right


def factor(gram):
    n = gram.shape[0]
    unit = (
        lax.broadcasted_iota(I32, (n, n), 0) == lax.broadcasted_iota(I32, (n, n), 1)
    ).astype(F32)
    lanes = lax.broadcasted_iota(I32, (SUB, n), 1)
    panel_rows = lax.broadcasted_iota(I32, (SUB, n), 0)
    left, right = gram[:SUB], unit[:SUB]
    rest, unit = gram[SUB:], unit[SUB:]
    uppers, inverses = [], []
    for at in range(0, n, SUB):
        more = at + SUB < n
        next_left, next_right = (rest[:SUB], unit[:SUB]) if more else (None, None)
        done_left, done_right, left, right = factor_panel(left, right, next_left, next_right, at)
        done_left = jnp.where(lanes >= panel_rows + at, done_left, 0.0)
        uppers.append(done_left)
        inverses.append(done_right)
        rest, unit = rest[SUB:], unit[SUB:]
        if at + 2 * SUB < n:
            h, m, l = split3(done_left)
            uh, um, ul = split3(done_right)
            terms = jnp.concatenate([h, h, m, h, l, m], 0)
            others = jnp.concatenate(
                [
                    jnp.concatenate([h, m, h, l, h, m], 0),
                    jnp.concatenate([uh, um, uh, ul, uh, um], 0),
                ],
                1,
            )
            change = jnp.dot(terms.T[at + 2 * SUB :], others, preferred_element_type=F32)
            rest = rest - change[:, :n]
            unit = unit - change[:, n:]
    return jnp.concatenate(uppers, 0), jnp.concatenate(inverses, 0)


def finish_kernel(gram_ref, far_ref, sketch_ref, q_ref, upper_ref):
    upper, inverse = factor(gram_ref[...] + far_ref[...])
    upper_ref[...] = upper
    q_ref[...] = lax.dot_general(
        sketch_ref[...],
        inverse,
        (((1,), (1,)), ((), ())),
        precision=lax.Precision.HIGHEST,
        preferred_element_type=F32,
    )


def per_device(features, sign_bits, sample_device, sample_offset):
    rows_dev, width = features.shape
    n_outer = lax.axis_size("exa")
    n_inner = lax.axis_size("exb")
    n_all = n_outer * n_inner
    bits = n_all.bit_length() - 1
    inner_bits = n_inner.bit_length() - 1
    myself = lax.axis_index("exa") * n_inner + lax.axis_index("exb")
    total = sample_offset.shape[0]
    own_count = total // n_all
    vmem = pl.BlockSpec(memory_space=pltpu.VMEM)

    def swap(value, mask):
        if mask < n_inner:
            return lax.ppermute(value, "exb", bit_perm(n_inner, mask))
        return lax.ppermute(value, "exa", bit_perm(n_outer, mask // n_inner))

    outer = tuple(range(inner_bits, bits))
    inner = [(bit,) for bit in range(1, inner_bits)]
    back = inner[::-1]
    orders = [(16, inner[:1] + [outer[:1]] + inner[1:] + [outer[1:]]), (16, back[:1] + [outer[:1]] + back[1:] + [outer[1:]]), (16, inner + [(bit,) for bit in outer]), (16, back + [(bit,) for bit in outer])]
    chunks, start = [], 0
    for share, steps in orders:
        chunks.append((start, own_count * share // 64, steps))
        start += own_count * share // 64

    def masks(step):
        listed = [0]
        for bit in step:
            listed = [e | 1 << bit for e in listed] + listed
        return listed

    def targets(steps):
        listed = [0]
        for step in steps[::-1]:
            listed = [m | e for m in masks(step) for e in listed]
        return listed

    firsts = []
    for start, count, steps in chunks:
        listed = targets(steps)
        moves = masks(steps[0])
        per = len(listed) // len(moves)
        firsts.append(
            [
                (listed[i * per : i * per + per], start, count)
                for i in range(len(moves))
            ]
        )
    flat = [piece for pieces in firsts for piece in pieces]

    far_features = swap(features, 1)
    far_signs = swap(sign_bits, 1)
    params = pltpu.CompilerParams(vmem_limit_bytes=22 * MIB)
    scratch = [
        pltpu.VMEM((rows_dev, width), F32),
        pltpu.VMEM((rows_dev, width), F32),
        pltpu.VMEM((rows_dev // PER_WORD, width), I32),
        pltpu.SemaphoreType.DMA((rows_dev // BLOCK,)),
    ]
    bits_shape = (rows_dev // 128, 128)
    place_shapes = [
        jax.ShapeDtypeStruct((1, len(which) * count), kind)
        for which, _, count in flat
        for kind in (I32, F32)
    ]
    own, *places = pl.pallas_call(
        functools.partial(own_kernel, 1.0 / math.sqrt(rows_dev * n_all), n_all, flat),
        out_shape=[jax.ShapeDtypeStruct((rows_dev, width), F32)] + place_shapes,
        in_specs=[
            pl.BlockSpec(memory_space=pl.ANY),
            vmem,
            pl.BlockSpec(memory_space=pltpu.SMEM),
            vmem,
            vmem,
        ],
        out_specs=[vmem] * (1 + len(place_shapes)),
        scratch_shapes=scratch,
        compiler_params=params,
        cost_estimate=pl.CostEstimate(flops=10**7, bytes_accessed=12 * MIB, transcendentals=0),
        name="own",
    )(
        pltpu.with_memory_space_constraint(features, pltpu.HBM),
        sign_bits.reshape(bits_shape),
        myself.reshape(1),
        sample_device.reshape(1, total),
        sample_offset.reshape(1, total),
    )
    table = pl.pallas_call(
        pair_kernel,
        out_shape=jax.ShapeDtypeStruct((2 * rows_dev, width), F32),
        in_specs=[pl.BlockSpec(memory_space=pl.ANY), vmem, vmem],
        out_specs=vmem,
        scratch_shapes=scratch,
        compiler_params=params,
        cost_estimate=pl.CostEstimate(flops=10**7, bytes_accessed=16 * MIB, transcendentals=0),
        name="pair",
    )(
        far_features,
        far_signs.reshape(bits_shape),
        pltpu.with_memory_space_constraint(own, pltpu.VMEM),
    )

    pairs = iter(zip(places[::2], places[1::2]))
    mine = [[next(pairs) for _ in pieces] for pieces in firsts]
    sent = [
        [swap(pick(one, table), mask) for one, mask in zip(some[:-1], masks(steps[0]))]
        for some, (_, _, steps) in zip(mine, chunks)
    ]
    waits = [None,None,0,1]
    kept = [
        pick(some[-1], table, () if wait is None else (sent[wait][0],))
        for some, wait in zip(mine, waits)
    ]
    for turn in range(1, max(len(steps) for _, _, steps in chunks) + 1):
        for n, (_, _, steps) in enumerate(chunks):
            if turn > len(steps):
                continue
            sums = functools.reduce(jnp.add, sent[n], kept[n])
            if turn < len(steps):
                listed = masks(steps[turn])
                per = sums.shape[0] // len(listed)
                sent[n] = [
                    swap(sums[i * per : i * per + per], move) for i, move in enumerate(listed[:-1])
                ]
                sums = sums[-per:]
            kept[n] = sums
    sketch = jnp.concatenate(kept, 0)

    gram = lax.dot_general(
        sketch,
        sketch,
        (((0,), (0,)), ((), ())),
        precision=lax.Precision.HIGHEST,
        preferred_element_type=F32,
    ) / total
    groups = [(0,)] + [tuple(range(b, min(b + 2, inner_bits))) for b in range(1, inner_bits, 2)]
    for group in groups + [(bit,) for bit in outer[1:]]:
        near = gram + swap(gram, 1 << group[0])
        if len(group) == 2:
            far = 1 << group[1]
            near = near + (swap(gram, far) + swap(gram, far | 1 << group[0]))
        gram = near

    return pl.pallas_call(
        finish_kernel,
        out_shape=(
            jax.ShapeDtypeStruct((own_count, width), F32),
            jax.ShapeDtypeStruct((width, width), F32),
        ),
        in_specs=[vmem, vmem, vmem],
        out_specs=(vmem, vmem),
        name="finish",
    )(gram, pltpu.with_memory_space_constraint(swap(gram, 1 << outer[0]), pltpu.VMEM), sketch)


def solution(mesh):
    placed = (P(("exa", "exb"), None), P(("exa", "exb")), P(), P())
    return jax.shard_map(
        per_device,
        mesh=mesh,
        in_specs=placed,
        out_specs=(P(("exa", "exb"), None), P()),
        check_vma=False,
    )
```
